256 devices in a mesh: group: 8 (over x_hi, y), blk: 32 (over x_lo, z, core).
Axes of the slice: x: 4 (x_hi: 2, x_lo: 2; x = x_hi * 2 + x_lo), y: 4, z: 8, core: 2. Of those that a mesh axis runs over, the one named last changes fastest.
Arguments:
- queries: bfloat16 [256, 24, 128], P(('group', 'blk')), may hold values from -0.59765625 to 0.59765625
- query_len: int32 [256], replicated, may hold values from 1 to 24
- pages: bfloat16 [1536, 1030, 128], P(('group', 'blk')), may hold values from -6 to 6
- page_count: int32 [768], P(('group', 'blk')), may hold values from 1 to 2, as said below
- page_offset: int32 [768], P(('group', 'blk')), may hold values from 0 to 4, as said below
- helper_doc: int32 [1536], P(('group', 'blk')), may hold values from -1 to 11, as said below
Outputs:
- scores: float32 [768, 256], P(('group', 'blk'))
The draws below stay inside these ranges and needn't reach their ends.
Inputs may be any that keep to these rules, and one draw needn't show every extreme that they name: `page_count`: every document has at least one home page; a device's home ranges do not intersect and lie back to back from slot 0, in an order of its own documents. `page_offset`: offsets are within the owner's slots and are consistent with page_count as stated there. helper_doc is -1 exactly on home slots; elsewhere it is s * 3 + j with 1 <= s <= 3. Home slots come before helper slots on each device.
All inputs are finite; a program needn't handle non-finite values.
Results may differ from the reference program's by a relative error of at most 0.0003.
Values may be sent and summed in bfloat16 or wider, within the bound.
No kernel may reach another device: no remote copies, remote signals or barrier semaphores. Data moves between devices by JAX's collectives and lax.ppermute only.
A program may use at most 64 MiB of HBM per device.

```python
import jax
import jax.numpy as jnp
from jax import lax

E = 128
PATCH = 1030
QTOK = 24
SPILL = 3
DOCS_DEV = 3
PAGES_DEV = 6
QUERIES = 256
DOCS = 768
PAGES = 1536
N_GROUP = 8
N_BLK = 32


def layout(key):
    device_count = DOCS // DOCS_DEV
    most = PAGES_DEV // DOCS_DEV
    key_counts = jax.random.fold_in(key, 11)
    key_order = jax.random.fold_in(key, 12)
    key_helpers = jax.random.fold_in(key, 13)
    counts = jax.random.randint(key_counts, (device_count, DOCS_DEV), 1, most + 1, dtype=jnp.int32)
    counts = counts.at[0].set(most)
    counts = counts.at[device_count - 1].set(1)
    subkeys = jax.random.split(key_order, device_count)
    orders = jax.vmap(lambda subkey: jax.random.permutation(subkey, DOCS_DEV))(subkeys).astype(jnp.int32)
    ranks = jnp.argsort(orders, axis=1).astype(jnp.int32)
    before = ranks[:, None, :] < ranks[:, :, None]
    offsets = jnp.sum(jnp.where(before, counts[:, None, :], 0), axis=2).astype(jnp.int32)
    home_total = jnp.sum(counts, axis=1)
    picks = jax.random.randint(key_helpers, (device_count, PAGES_DEV), DOCS_DEV, (SPILL + 1) * DOCS_DEV, dtype=jnp.int32)
    picks = picks.at[device_count - 1, PAGES_DEV - 1].set((SPILL + 1) * DOCS_DEV - 1)
    slots = jnp.arange(PAGES_DEV, dtype=jnp.int32)[None, :]
    helpers = jnp.where(slots >= home_total[:, None], picks, -1).astype(jnp.int32)
    return (counts.reshape(-1), offsets.reshape(-1), helpers.reshape(-1))


def draw_page_count(key, part):
    counts, offsets, helpers = layout(key)
    return counts


def draw_page_offset(key, part):
    counts, offsets, helpers = layout(key)
    return offsets


def draw_helper_doc(key, part):
    counts, offsets, helpers = layout(key)
    return helpers


def touch_ends(array, own_key, low, largest):
    spot = [jax.random.randint(jax.random.fold_in(own_key, axis), (), 0, length) for axis, length in enumerate(array.shape)]
    main_axis = array.shape.index(max(array.shape))
    beside = spot[:main_axis] + [(spot[main_axis] + 1) % array.shape[main_axis]] + spot[main_axis + 1:]
    return array.at[tuple(spot)].set(low).at[tuple(beside)].set(largest)


def steps_of(stream_key, extent, cuts, smallest, largest):
    gain = 1.0
    for axis_at, blocks in cuts:
        heights = jax.random.uniform(jax.random.fold_in(jax.random.fold_in(stream_key, 6), axis_at), (blocks,), jnp.float32, smallest / len(cuts), largest / len(cuts))
        gain = gain * jnp.repeat(jnp.exp(heights), extent[axis_at] // blocks).reshape((-1,) + (1,) * (len(extent) - 1 - axis_at))
    return gain


def normal_values(stream_key, extent, spread, most, pieces=(), kind=jnp.bfloat16):
    entries = jax.random.normal(stream_key, extent, jnp.float32) * spread
    if len(pieces) > 0:
        entries = steps_of(stream_key, extent, pieces, -0.22, 0.18) * entries
    return jnp.clip(entries, min=-most, max=most).astype(kind)


def setup_inputs(seed: int = 0) -> dict:
    key_of = jax.random.split(jax.random.key(seed), 7)
    return {
        "queries": normal_values(key_of[0], (QUERIES, QTOK, E), 0.088, 0.59765625, ((0, 256),)),
        "query_len": touch_ends(jax.random.randint(key_of[1], (QUERIES,), 1, QTOK + 1), jax.random.fold_in(key_of[1], 1), 1, QTOK).astype(jnp.int32),
        "pages": normal_values(key_of[2], (PAGES, PATCH, E), 1.0, 6.0, ((0, 256),)),
        "page_count": draw_page_count(jax.random.fold_in(key_of[6], 71), 0),
        "page_offset": draw_page_offset(jax.random.fold_in(key_of[6], 71), 0),
        "helper_doc": draw_helper_doc(jax.random.fold_in(key_of[6], 71), 0),
    }


lowest = -1.0e30


def reference(queries, query_len, pages, page_count, page_offset, helper_doc):
    devices_all = N_GROUP * N_BLK
    token_cols = queries.reshape(QUERIES * QTOK, E).T
    counts = page_count.reshape(devices_all, DOCS_DEV)
    offsets = page_offset.reshape(devices_all, DOCS_DEV)
    helpers = helper_doc.reshape(devices_all, PAGES_DEV)
    positions = jnp.arange(PAGES_DEV, dtype=jnp.int32)[None, None, :]
    inside = (positions >= offsets[:, :, None]) & (positions < offsets[:, :, None] + counts[:, :, None])
    home_doc = jnp.sum(jnp.where(inside, jnp.arange(DOCS_DEV, dtype=jnp.int32)[None, :, None], 0), axis=1)
    is_home = jnp.any(inside, axis=1)
    device_ids = jnp.arange(devices_all, dtype=jnp.int32)[:, None]
    group_index = device_ids // N_BLK
    blk_index = device_ids % N_BLK
    distance = jnp.where(is_home, 0, helpers // DOCS_DEV)
    local_doc = jnp.where(is_home, home_doc, helpers % DOCS_DEV)
    owner = group_index * N_BLK + (blk_index - distance) % N_BLK
    doc_ids = (owner * DOCS_DEV + local_doc).reshape(-1).astype(jnp.int32)

    def visit(table, item):
        page_rows, doc_id = item
        scores = jnp.dot(page_rows, token_cols, preferred_element_type=jnp.float32)
        patch_best = jnp.max(scores, axis=0)
        current = lax.dynamic_index_in_dim(table, doc_id, 0, keepdims=False)
        table = lax.dynamic_update_index_in_dim(table, jnp.maximum(current, patch_best), doc_id, 0)
        return table, None

    start_table = jnp.full((DOCS, QUERIES * QTOK), lowest, jnp.float32)
    table, unused = lax.scan(visit, start_table, (pages, doc_ids))
    table = table.reshape(DOCS, QUERIES, QTOK)
    valid = jnp.arange(QTOK, dtype=jnp.int32)[None, :] < query_len[:, None]
    totals = jnp.sum(jnp.where(valid[None], table, jnp.float32(0.0)), axis=2)
    return totals / query_len.astype(jnp.float32)[None, :]
```

```python
import jax
import jax.numpy as jnp
from jax import lax
from jax.experimental import pallas as pl
from jax.experimental.pallas import tpu as pltpu
from jax.sharding import Mesh, PartitionSpec as P

SPILL = 3
SIZES = (2, 4, 2, 8, 2)
AXES = ("xh", "y", "xl", "z", "c")
NX, NY, NZ, NC = 4, 4, 8, 2
CHUNK = NY * NZ
TILE = 512
lowest = -1e30
VMEM_LIMIT = 48 * 1024 * 1024
TRANSPOSED = (((1,), (1,)), ((), ()))


def device_id(x, y, z, c):
    return (((x // 2) * NY + y) * 2 + x % 2) * NZ * NC + z * NC + c


def coordinates():
    return [
        (x, y, z, c) for x in range(NX) for y in range(NY) for z in range(NZ) for c in range(NC)
    ]


def along_x(value, steps):
    pairs = [
        (device_id(x, y, z, c), device_id((x + steps) % NX, y, z, c)) for x, y, z, c in coordinates()
    ]
    return lax.ppermute(value, AXES, pairs)


def other_core(value):
    pairs = [(device_id(x, y, z, c), device_id(x, y, z, 1 - c)) for x, y, z, c in coordinates()]
    return lax.ppermute(value, AXES, pairs)


def along_blk(value, steps):
    count = 32
    pairs = [
        (g * count + b, g * count + (b + steps) % count) for g in range(8) for b in range(count)
    ]
    return lax.ppermute(value, AXES, pairs)


def query_index(x, c, k):
    return device_id(x, k // NZ, k % NZ, c)


def slot_ids(count_ref, offset_ref, helper_ref, pages):
    ids = []
    for k in range(pages):
        slot = helper_ref[k]
        for j in range(count_ref.shape[0]):
            inside = (offset_ref[j] <= k) & (k < offset_ref[j] + count_ref[j])
            slot = jnp.where(inside, j, slot)
        ids.append(jnp.clip(slot, 0, (SPILL + 1) * count_ref.shape[0] - 1))
    return ids


def maxima_kernel(len_ref, count_ref, offset_ref, helper_ref, *rest):
    chunks = rest[: NX * NC]
    pages_ref = rest[NX * NC]
    outs = rest[NX * NC + 1 : NX * NC + 2 + SPILL]
    live_ref, tail_ref, slot_ref = rest[NX * NC + 2 + SPILL :]
    pages, patches, width = pages_ref.shape
    docs = count_ref.shape[0]
    whole = patches // 16 * 16
    rest_rows = patches - whole
    tokens = chunks[0].shape[1]

    for p in range(pages):
        tail_ref[8 * p : 8 * p + rest_rows, :] = pages_ref[p, whole:, :].astype(jnp.float32)
        for extra in range(rest_rows, 8):
            tail_ref[8 * p + extra : 8 * p + extra + 1, :] = pages_ref[
                p, patches - 1 : patches, :
            ].astype(jnp.float32)
    tails = tail_ref[...].astype(jnp.bfloat16)

    x = lax.axis_index("xh") * 2 + lax.axis_index("xl")
    c = lax.axis_index("c")
    totals = []
    for chunk in range(NX * NC):

        def add(k, total, chunk=chunk):
            return total + len_ref[query_index(chunk // NC, chunk % NC, k)]

        totals.append(lax.fori_loop(0, CHUNK, add, jnp.int32(0), unroll=8))
    total = sum(totals)

    for place, steps in enumerate((0, 1, 3, 2)):
        for core in range(NC):
            source = chunks[place * NC + core]
            chunk_x = lax.rem(x + NX - steps, NX)
            chunk_c = c if core == 0 else 1 - c
            chunk_id = chunk_x * NC + chunk_c
            start = jnp.int32(0)
            for other in range(NX * NC):
                start = start + jnp.where(other < chunk_id, totals[other], 0)

            end = start
            for other in range(NX * NC):
                end = end + jnp.where(other == chunk_id, totals[other], 0)
            after = live_ref[pl.ds(end, tokens), :]

            def put(k, at, source=source, chunk_x=chunk_x, chunk_c=chunk_c):
                live_ref[pl.ds(at, tokens), :] = source[k].astype(jnp.float32)
                return at + len_ref[query_index(chunk_x, chunk_c, k)]

            lax.fori_loop(0, CHUNK, put, start, unroll=8)
            live_ref[pl.ds(end, tokens), :] = after
    live_ref[pl.ds(total, TILE), :] = jnp.zeros((TILE, width), jnp.float32)

    ids = slot_ids(count_ref, offset_ref, helper_ref, pages)

    def visit(tile, _):
        at = pl.multiple_of(tile * TILE, TILE)
        token_rows = live_ref[pl.ds(at, TILE), :].astype(jnp.bfloat16)
        tail_scores = lax.dot_general(
            tails, token_rows, TRANSPOSED, preferred_element_type=jnp.float32
        )
        slot_ref[...] = jnp.full(slot_ref.shape, lowest, jnp.float32)
        for p in range(pages):
            scores = lax.dot_general(
                pages_ref[p, :whole, :], token_rows, TRANSPOSED, preferred_element_type=jnp.float32
            )
            best = jnp.max(scores.reshape(whole // 8, 8, TILE), axis=0)
            best = jnp.maximum(best, tail_scores[8 * p : 8 * p + 8])
            best = jnp.max(best, axis=0, keepdims=True)
            slot_ref[ids[p]] = jnp.maximum(slot_ref[ids[p]], best)
        for distance in range(SPILL + 1):
            for j in range(docs):
                outs[distance][j, :, pl.ds(at, TILE)] = slot_ref[distance * docs + j]
        return 0

    lax.fori_loop(0, (total + TILE - 1) // TILE, visit, 0)


def scores_kernel(len_ref, own_ref, one_ref, two_ref, three_ref, out_ref, acc_ref):
    queries = len_ref.shape[1]
    docs = own_ref.shape[0]
    lens = len_ref[...]

    def place(n):
        core = n % NC
        z = (n // NC) % NZ
        x_lo = (n // (NC * NZ)) % 2
        y = (n // (NC * NZ * 2)) % NY
        x_hi = n // (NC * NZ * 2 * NY)
        return (((x_hi * 2 + x_lo) * NC + core) * NY + y) * NZ + z

    before = place(lax.broadcasted_iota(jnp.int32, (queries, queries), 0)) < place(
        lax.broadcasted_iota(jnp.int32, (queries, queries), 1)
    )
    row = jnp.broadcast_to(lens.astype(jnp.float32).astype(jnp.bfloat16), (8, queries))
    starts = jnp.dot(
        row,
        jnp.where(before, 1.0, 0.0).astype(jnp.bfloat16),
        preferred_element_type=jnp.float32,
    )[0:1].astype(jnp.int32)
    ends = starts + lens
    total = jnp.max(ends)
    acc_ref[...] = jnp.zeros(acc_ref.shape, jnp.float32)

    def visit(tile, _):
        at = pl.multiple_of(tile * TILE, TILE)
        columns = lax.broadcasted_iota(jnp.int32, (1, TILE), 1) + at
        parts = []
        for j in range(docs):
            value = jnp.maximum(
                jnp.maximum(own_ref[j, :, pl.ds(at, TILE)], one_ref[j, :, pl.ds(at, TILE)]),
                jnp.maximum(two_ref[j, :, pl.ds(at, TILE)], three_ref[j, :, pl.ds(at, TILE)]),
            )
            value = jnp.where(columns < total, value, 0.0)
            high = value.astype(jnp.bfloat16)
            left = value - high.astype(jnp.float32)
            middle = left.astype(jnp.bfloat16)
            low = (left - middle.astype(jnp.float32)).astype(jnp.bfloat16)
            parts += [high.astype(jnp.float32), middle.astype(jnp.float32), low.astype(jnp.float32)]
        parts.append(jnp.zeros((acc_ref.shape[0] - len(parts), TILE), jnp.float32))
        left_side = jnp.concatenate(parts, axis=0).astype(jnp.bfloat16)
        token = lax.broadcasted_iota(jnp.int32, (TILE, queries), 0) + at
        chosen = jnp.where((token >= starts) & (token < ends), 1.0, 0.0).astype(jnp.bfloat16)
        acc_ref[...] += jnp.dot(left_side, chosen, preferred_element_type=jnp.float32)
        return 0

    lax.fori_loop(0, (total + TILE - 1) // TILE, visit, 0)
    divisor = lens.astype(jnp.float32)
    for j in range(docs):
        summed = (acc_ref[3 * j : 3 * j + 1, :] + acc_ref[3 * j + 1 : 3 * j + 2, :]) + acc_ref[
            3 * j + 2 : 3 * j + 3, :
        ]
        out_ref[j : j + 1, :] = summed / divisor


SMEM = pl.BlockSpec(memory_space=pltpu.SMEM)
VMEM = pl.BlockSpec(memory_space=pltpu.VMEM)


def local(queries, query_len, pages, page_count, page_offset, helper_doc):
    docs = page_count.shape[0]
    total = query_len.shape[0]
    tokens, width = queries.shape[1:]
    columns = total * tokens

    copies = jnp.broadcast_to(queries, (CHUNK, tokens, width))
    mine = lax.all_to_all(copies, ("y", "z"), 0, 0, tiled=True)
    chunks = []
    for steps in (0, 1, 3, 2):
        value = mine if steps == 0 else along_x(mine, steps)
        chunks += [value, other_core(value)]

    maxima = pl.pallas_call(
        maxima_kernel,
        out_shape=[jax.ShapeDtypeStruct((docs, 1, columns), jnp.float32)] * (SPILL + 1),
        in_specs=[SMEM] * 4 + [VMEM] * (len(chunks) + 1),
        out_specs=[VMEM] * (SPILL + 1),
        scratch_shapes=[
            pltpu.VMEM((columns + TILE, width), jnp.float32),
            pltpu.VMEM((8 * pages.shape[0], width), jnp.float32),
            pltpu.VMEM(((SPILL + 1) * docs, 1, TILE), jnp.float32),
        ],
        compiler_params=pltpu.CompilerParams(vmem_limit_bytes=VMEM_LIMIT),
    )(query_len, page_count, page_offset, helper_doc, *chunks, pages)

    arrived = [along_blk(maxima[distance], -distance) for distance in range(1, SPILL + 1)]
    return pl.pallas_call(
        scores_kernel,
        out_shape=jax.ShapeDtypeStruct((docs, total), jnp.float32),
        in_specs=[VMEM] * (SPILL + 2),
        out_specs=VMEM,
        scratch_shapes=[pltpu.VMEM((16, total), jnp.float32)],
        compiler_params=pltpu.CompilerParams(vmem_limit_bytes=VMEM_LIMIT),
    )(query_len[None, :], maxima[0], *arrived)


def solution(mesh):
    split = Mesh(mesh.devices.reshape(SIZES), AXES)
    return jax.shard_map(
        local,
        mesh=split,
        in_specs=(P(AXES, None, None), P(), P(AXES, None, None), P(AXES), P(AXES), P(AXES)),
        out_specs=P(AXES, None),
        check_vma=False,
    )
```

```python
import functools

import jax
import jax.numpy as jnp
from jax import lax
from jax.experimental import pallas as pl
from jax.experimental.pallas import tpu as pltpu
from jax.sharding import Mesh, PartitionSpec as P

SPILL = 3
SIZES = (2, 4, 2, 8, 2)
AXES = ("xh", "y", "xl", "z", "c")
NX, NY, NZ, NC = 4, 4, 8, 2
CHUNK = NY * NZ
TILE = 256
lowest = -1e30
VMEM_LIMIT = 48 * 1024 * 1024
TRANSPOSED = (((1,), (1,)), ((), ()))


def device_id(x, y, z, c):
    return (((x // 2) * NY + y) * 2 + x % 2) * NZ * NC + z * NC + c


def coordinates():
    return [
        (x, y, z, c) for x in range(NX) for y in range(NY) for z in range(NZ) for c in range(NC)
    ]


def along_x(value, steps):
    pairs = [
        (device_id(x, y, z, c), device_id((x + steps) % NX, y, z, c)) for x, y, z, c in coordinates()
    ]
    return lax.ppermute(value, AXES, pairs)


def other_core(value):
    pairs = [(device_id(x, y, z, c), device_id(x, y, z, 1 - c)) for x, y, z, c in coordinates()]
    return lax.ppermute(value, AXES, pairs)


def along_blk(value, steps):
    count = 32
    pairs = [
        (g * count + b, g * count + (b + steps) % count) for g in range(8) for b in range(count)
    ]
    return lax.ppermute(value, AXES, pairs)


def region_of(x_abs, core):
    return (x_abs // 2) * (NY * 2 * NZ * NC) + (x_abs % 2) * (NZ * NC) + core


PLACES = [y * (2 * NZ * NC) + z * NC for y in range(NY) for z in range(NZ)]


def chunk_total(len_ref, x_abs, core):
    first = region_of(x_abs, core)
    terms = [len_ref[first + place] for place in PLACES]
    while len(terms) > 1:
        terms = [sum(terms[i : i + 2]) for i in range(0, len(terms), 2)]
    return terms[0]


def chunk_of(spec, x, c):
    steps, core = spec
    return lax.rem(x + NX - steps, NX), (c if core == 0 else 1 - c)


def compact(len_ref, live_ref, base, chunk, source):
    tokens = source.shape[1]
    first = region_of(*chunk)
    at = base
    for k, place in enumerate(PLACES):
        live_ref[pl.ds(at, tokens), :] = source[k].astype(jnp.float32)
        at = at + len_ref[first + place]
    return at - base


def slot_ids(count_ref, offset_ref, helper_ref, pages):
    docs = count_ref.shape[0]
    ids = []
    for k in pages:
        slot = jnp.int32(0) if helper_ref is None else helper_ref[k]
        for j in range(docs):
            inside = (offset_ref[j] <= k) & (k < offset_ref[j] + count_ref[j])
            slot = jnp.where(inside, j, slot)
        ids.append(jnp.clip(slot, 0, (SPILL + 1) * docs - 1))
    return ids


def fill_tails(pages_ref, tail_ref):
    pages, patches, _ = pages_ref.shape
    whole = patches // 16 * 16
    tail_ref[...] = jnp.zeros(tail_ref.shape, jnp.float32)
    for p in range(pages):
        tail_ref[8 * p : 8 * p + patches - whole, :] = pages_ref[p, whole:, :].astype(jnp.float32)
        for extra in range(patches - whole, 8):
            tail_ref[8 * p + extra : 8 * p + extra + 1, :] = pages_ref[
                p, patches - 1 : patches, :
            ].astype(jnp.float32)
    return tail_ref[...].astype(jnp.bfloat16)


def page_best(token_rows, pages_ref, tails):
    pages, patches, _ = pages_ref.shape
    whole = patches // 16 * 16
    columns = token_rows.shape[0]
    tail_scores = lax.dot_general(
        tails, token_rows, TRANSPOSED, preferred_element_type=jnp.float32
    )
    rows = []
    for p in range(pages):
        scores = lax.dot_general(
            pages_ref[p, :whole, :], token_rows, TRANSPOSED, preferred_element_type=jnp.float32
        )
        best = jnp.max(scores.reshape(whole // 8, 8, columns), axis=0)
        best = jnp.maximum(best, tail_scores[8 * p : 8 * p + 8])
        rows.append(jnp.max(best, axis=0, keepdims=True))
    return rows


def over_tiles(total, visit):
    tiles = (total + TILE - 1) // TILE

    def double(i, _):
        visit(pl.multiple_of(i * (2 * TILE), 2 * TILE), 2 * TILE)
        return 0

    lax.fori_loop(0, tiles // 2, double, 0)

    @pl.when(tiles % 2 == 1)
    def _():
        visit(pl.multiple_of((tiles - 1) * TILE, TILE), TILE)


def own_position():
    return lax.axis_index("xh") * 2 + lax.axis_index("xl"), lax.axis_index("c")


def all_slots(live_ref, base, at, size, ids, pages_ref, tails, slot_ref, outs, write):
    token_rows = live_ref[pl.ds(base + at, size), :].astype(jnp.bfloat16)
    slot_ref[...] = jnp.full(slot_ref.shape, lowest, jnp.float32)
    for slot, best in zip(ids, page_best(token_rows, pages_ref, tails)):
        slot_ref[slot, :, :size] = jnp.maximum(slot_ref[slot, :, :size], best)
    docs = outs[0].shape[0]
    for distance in range(SPILL + 1):
        for j in range(docs):
            write(outs[distance], j, slot_ref[distance * docs + j, :, :size])
    return token_rows


def whole_chunks(specs, plan_ref, sources, outs, pages_ref, live_ref, slot_ref, ids, tails):
    x, c = own_position()
    room = live_ref.shape[0] // len(specs)
    totals = [
        compact(plan_ref, live_ref, i * room, chunk_of(spec, x, c), source)
        for i, (spec, source) in enumerate(zip(specs, sources))
    ]
    for i in range(len(specs)):

        def visit(at, size, i=i):
            def write(out, j, value):
                out[j, i, :, pl.ds(at, size)] = value

            all_slots(live_ref, i * room, at, size, ids, pages_ref, tails, slot_ref, outs, write)

        over_tiles(totals[i], visit)


def first_kernel(specs, len_hbm, count_hbm, offset_hbm, helper_hbm, *rest):
    sources, rest = rest[: len(specs)], rest[len(specs) :]
    pages_ref, rest = rest[0], rest[1:]
    outs, rest = rest[: SPILL + 1], rest[SPILL + 1 :]
    plan_ref, count_ref, offset_ref, helper_ref, live_ref, tail_ref, slot_ref, sem = rest
    pages = pages_ref.shape[0]
    moves = [
        pltpu.make_async_copy(source, target, sem.at[i])
        for i, (source, target) in enumerate(
            (
                (len_hbm, plan_ref.at[pl.ds(0, len_hbm.shape[0])]),
                (count_hbm, count_ref),
                (offset_hbm, offset_ref),
                (helper_hbm, helper_ref),
            )
        )
    ]
    for move in moves:
        move.start()
    tails = fill_tails(pages_ref, tail_ref)
    for move in moves:
        move.wait()
    ids = slot_ids(count_ref, offset_ref, helper_ref, range(pages))
    at = len_hbm.shape[0]
    for k in range(pages):
        plan_ref[at + k] = ids[k]
    for chunk in range(NX * NC):
        plan_ref[at + pages + chunk] = chunk_total(plan_ref, chunk // NC, chunk % NC)
    whole_chunks(specs, plan_ref, sources, outs, pages_ref, live_ref, slot_ref, ids, tails)


def more_kernel(specs, queries, plan_ref, *rest):
    sources, rest = rest[: len(specs)], rest[len(specs) :]
    pages_ref, rest = rest[0], rest[1:]
    outs, rest = rest[: SPILL + 1], rest[SPILL + 1 :]
    live_ref, tail_ref, slot_ref = rest
    ids = [plan_ref[queries + k] for k in range(pages_ref.shape[0])]
    tails = fill_tails(pages_ref, tail_ref)
    whole_chunks(specs, plan_ref, sources, outs, pages_ref, live_ref, slot_ref, ids, tails)


def chunk_count(plan_ref, chunk):
    return plan_ref[plan_ref.shape[0] - NX * NC + chunk[0] * NC + chunk[1]]


def most_tokens(plan_ref):
    most = plan_ref[plan_ref.shape[0] - NX * NC]
    for chunk in range(1, NX * NC):
        most = jnp.maximum(most, plan_ref[plan_ref.shape[0] - NX * NC + chunk])
    return most


def chosen_kernel(plan_ref, lens_ref, chosen_ref):
    span = chosen_ref.shape[0] // (NX * NC)
    half = chosen_ref.shape[1]
    starts, ends = query_columns(lens_ref[...], span)

    def step(tile, _):
        for chunk in range(NX * NC):
            lanes = slice(chunk // (2 * NC) * half, (chunk // (2 * NC) + 1) * half)
            first = pl.multiple_of(chunk * span + tile * TILE, TILE)
            token = lax.broadcasted_iota(jnp.int32, (TILE, half), 0) + first
            inside = (token >= starts[:, lanes]) & (token < ends[:, lanes])
            chosen_ref[pl.ds(first, TILE), :] = jnp.where(inside, 1.0, 0.0).astype(jnp.bfloat16)
        return 0

    lax.fori_loop(0, (most_tokens(plan_ref) + TILE - 1) // TILE, step, 0)


def query_columns(lens, span):
    queries = lens.shape[1]

    def chunk(n):
        return ((n // (NC * NZ * 2 * NY)) * 2 + (n // (NC * NZ)) % 2) * NC + n % NC

    def place(n):
        return (n // (NC * NZ * 2)) % NY * NZ + (n // NC) % NZ

    one = lax.broadcasted_iota(jnp.int32, (queries, queries), 0)
    two = lax.broadcasted_iota(jnp.int32, (queries, queries), 1)
    before = (chunk(one) == chunk(two)) & (place(one) < place(two))
    row = jnp.broadcast_to(lens.astype(jnp.float32).astype(jnp.bfloat16), (16, queries))
    starts = jnp.dot(
        row,
        jnp.where(before, 1.0, 0.0).astype(jnp.bfloat16),
        preferred_element_type=jnp.float32,
    )[0:1].astype(jnp.int32)
    starts = starts + chunk(lax.broadcasted_iota(jnp.int32, (1, queries), 1)) * span
    return starts, starts + lens


def late_kernel(specs, placed, queries, plan_ref, *rest):
    sources, rest = rest[: len(specs)], rest[len(specs) :]
    all_pages_ref, rest = rest[0], rest[1:]
    before, rest = rest[: len(placed) * (SPILL + 1)], rest[len(placed) * (SPILL + 1) :]
    outs, rest = rest[: SPILL + 1], rest[SPILL + 1 :]
    kept_ref, live_ref, tail_ref, slot_ref = rest
    docs = outs[0].shape[0]
    pages = all_pages_ref.shape[0]
    pages_ref = all_pages_ref.at[pl.ds(docs, pages - docs)]
    x, c = own_position()
    room = kept_ref.shape[1]
    span = outs[0].shape[2] // (NX * NC)

    def column(spec):
        chunk = chunk_of(spec, x, c)
        return pl.multiple_of((chunk[0] * NC + chunk[1]) * span, TILE)

    for group, group_specs in enumerate(placed):
        for i, spec in enumerate(group_specs):
            for distance in range(SPILL + 1):
                for j in range(docs):
                    outs[distance][j, :, pl.ds(column(spec), span)] = before[
                        group * (SPILL + 1) + distance
                    ][j, i]
    ids = [plan_ref[queries + k] for k in range(docs, pages)]
    tails = fill_tails(pages_ref, tail_ref)
    totals = [
        compact(plan_ref, live_ref, i * room, chunk_of(spec, x, c), source)
        for i, (spec, source) in enumerate(zip(specs, sources))
    ]
    for i, spec in enumerate(specs):
        where = column(spec)

        def visit(at, size, i=i, where=where):
            to = pl.multiple_of(where + at, TILE)

            def write(out, j, value):
                out[j, :, pl.ds(to, size)] = value

            kept_ref[i, pl.ds(at, size), :] = all_slots(
                live_ref, i * room, at, size, ids, pages_ref, tails, slot_ref, outs, write
            )

        over_tiles(totals[i], visit)


def home_kernel(specs, queries, plan_ref, kept_ref, all_pages_ref, before_ref, out_ref, tail_ref):
    docs, _, _, span = out_ref.shape
    pages_ref = all_pages_ref.at[pl.ds(0, docs)]
    x, c = own_position()
    ids = [plan_ref[queries + k] for k in range(docs)]
    tails = fill_tails(pages_ref, tail_ref)
    for i, spec in enumerate(specs):
        chunk = chunk_of(spec, x, c)
        where = pl.multiple_of((chunk[0] * NC + chunk[1]) * span, TILE)

        def visit(at, size, i=i, where=where):
            to = pl.multiple_of(where + at, TILE)
            rows = page_best(kept_ref[i, pl.ds(at, size), :], pages_ref, tails)
            for j in range(docs):
                out_ref[j, i, :, pl.ds(at, size)] = before_ref[j, :, pl.ds(to, size)]
            for slot, best in zip(ids, rows):
                out_ref[slot, i, :, pl.ds(at, size)] = jnp.maximum(
                    out_ref[slot, i, :, pl.ds(at, size)], best
                )

        over_tiles(chunk_count(plan_ref, chunk), visit)


def scores_kernel(groups, plan_ref, lens_ref, chosen_ref, *rest):
    homes, rest = rest[: len(groups)], rest[len(groups) :]
    received, (out_ref, acc_ref) = rest[:SPILL], rest[SPILL:]
    docs, _, columns_all = received[0].shape
    lens = lens_ref[...]
    span = columns_all // (NX * NC)
    x, c = own_position()
    acc_ref[...] = jnp.zeros(acc_ref.shape, jnp.float32)
    parts_list = [
        (home, i, chunk_of(spec, x, c))
        for home, group in zip(homes, groups)
        for i, spec in enumerate(group)
    ]

    def visit(at, size):
        for home_ref, i, chunk in parts_list:
            to = pl.multiple_of((chunk[0] * NC + chunk[1]) * span + at, TILE)
            total = chunk_count(plan_ref, chunk)
            live = lax.broadcasted_iota(jnp.int32, (1, size), 1) + at < total
            parts = []
            for j in range(docs):
                value = home_ref[j, i, :, pl.ds(at, size)]
                for ref in received:
                    value = jnp.maximum(value, ref[j, :, pl.ds(to, size)])
                value = jnp.where(live, value, 0.0)
                high = value.astype(jnp.bfloat16).astype(jnp.float32)
                left = value - high
                middle = left.astype(jnp.bfloat16).astype(jnp.float32)
                parts += [high, middle, left - middle]
            parts.append(jnp.zeros((acc_ref.shape[1] - len(parts), size), jnp.float32))
            left_side = jnp.concatenate(parts, axis=0).astype(jnp.bfloat16)
            x_hi = chunk[0] // 2
            acc_ref[x_hi] = acc_ref[x_hi] + jnp.dot(
                left_side, chosen_ref[pl.ds(to, size), :], preferred_element_type=jnp.float32
            )

    over_tiles(most_tokens(plan_ref), visit)
    half = acc_ref.shape[2]
    for x_hi in range(acc_ref.shape[0]):
        lanes = slice(x_hi * half, (x_hi + 1) * half)
        divisor = lens[:, lanes].astype(jnp.float32)
        for j in range(docs):
            high, middle, low = (acc_ref[x_hi, 3 * j + i : 3 * j + i + 1, :] for i in range(3))
            out_ref[j : j + 1, lanes] = ((high + middle) + low) / divisor


SMEM = pl.BlockSpec(memory_space=pltpu.SMEM)
VMEM = pl.BlockSpec(memory_space=pltpu.VMEM)
HBM = pl.BlockSpec(memory_space=pltpu.HBM)


def copies_kernel(block_ref, out_ref):
    for i in range(out_ref.shape[0]):
        out_ref[i] = block_ref[0]


def local(queries, query_len, pages, page_count, page_offset, helper_doc):
    docs = page_count.shape[0]
    total = query_len.shape[0]
    tokens, width = queries.shape[1:]
    columns = total * tokens
    span = columns // (NX * NC)
    room = span + TILE
    params = pltpu.CompilerParams(vmem_limit_bytes=VMEM_LIMIT)
    whole = [jax.ShapeDtypeStruct((docs, 1, columns), jnp.float32)] * (SPILL + 1)
    slots = pltpu.VMEM(((SPILL + 1) * docs, 1, 2 * TILE), jnp.float32)
    row = query_len[None, :]
    own, far, rest = [(0, 0), (0, 1)], [(2, 0)], [(2, 1), (1, 0), (1, 1), (3, 0), (3, 1)]

    def part(specs):
        return [jax.ShapeDtypeStruct((docs, len(specs), 1, span), jnp.float32)] * (SPILL + 1)

    def tail_room(count):
        return pltpu.VMEM((8 * count + 8 * count % 16, width), jnp.float32)

    def live_room(specs):
        return pltpu.VMEM((len(specs) * room, width), jnp.float32)

    def cost(rows):
        return pl.CostEstimate(
            flops=2 * rows * columns * width, bytes_accessed=rows * width * 2, transcendentals=0
        )

    copies = pl.pallas_call(
        copies_kernel,
        out_shape=jax.ShapeDtypeStruct((CHUNK, tokens, width), jnp.bfloat16),
        in_specs=[VMEM],
        out_specs=VMEM,
        cost_estimate=cost(pages.shape[0] * pages.shape[1]),
    )(queries)
    mine = lax.all_to_all(copies, ("y", "z"), 0, 0, tiled=True)
    mine_other = other_core(mine)
    two, one, three = [along_x(mine, steps) for steps in (2, 1, 3)]

    *own_out, plan = pl.pallas_call(
        functools.partial(first_kernel, own),
        out_shape=part(own)
        + [jax.ShapeDtypeStruct((total + pages.shape[0] + NX * NC,), jnp.int32)],
        in_specs=[HBM] * 4 + [VMEM] * (len(own) + 1),
        out_specs=[VMEM] * (SPILL + 1) + [SMEM],
        scratch_shapes=[
            pltpu.SMEM(page_count.shape, jnp.int32),
            pltpu.SMEM(page_offset.shape, jnp.int32),
            pltpu.SMEM(helper_doc.shape, jnp.int32),
            live_room(own),
            tail_room(pages.shape[0]),
            slots,
            pltpu.SemaphoreType.DMA((4,)),
        ],
        compiler_params=params,
        cost_estimate=cost(700),
    )(query_len, page_count, page_offset, helper_doc, mine, mine_other, pages)

    two, plan = lax.optimization_barrier((two, plan))
    far_out = pl.pallas_call(
        functools.partial(more_kernel, far, total),
        out_shape=part(far),
        in_specs=[SMEM] + [VMEM] * (len(far) + 1),
        out_specs=[VMEM] * (SPILL + 1),
        scratch_shapes=[live_room(far), tail_room(pages.shape[0]), slots],
        compiler_params=params,
        cost_estimate=cost(700),
    )(plan, two, pages)

    one, two, three, far_out = lax.optimization_barrier((one, two, three, far_out))
    two_other, one_other, three_other = [other_core(value) for value in (two, one, three)]
    chosen = pl.pallas_call(
        chosen_kernel,
        out_shape=jax.ShapeDtypeStruct((columns, total // 2), jnp.bfloat16),
        in_specs=[SMEM, VMEM],
        out_specs=VMEM,
        compiler_params=params,
        cost_estimate=cost(pages.shape[1]),
    )(plan, row)
    arrived = [two_other, one, one_other, three, three_other]
    *arrived, chosen = lax.optimization_barrier((*arrived, chosen))

    *partials, kept = pl.pallas_call(
        functools.partial(late_kernel, rest, (own, far), total),
        out_shape=whole + [jax.ShapeDtypeStruct((len(rest), room, width), jnp.bfloat16)],
        in_specs=[SMEM] + [VMEM] * (len(rest) + 1 + 2 * (SPILL + 1)),
        out_specs=[VMEM] * (SPILL + 2),
        scratch_shapes=[live_room(rest), tail_room(pages.shape[0] - docs), slots],
        compiler_params=params,
        cost_estimate=cost((pages.shape[0] - docs) * pages.shape[1]),
    )(plan, *arrived, pages, *own_out, *far_out)
    received = [along_blk(partials[distance], -distance) for distance in range(1, SPILL + 1)]

    rest_home = pl.pallas_call(
        functools.partial(home_kernel, rest, total),
        out_shape=part(rest)[0],
        in_specs=[SMEM] + [VMEM] * 3,
        out_specs=VMEM,
        scratch_shapes=[tail_room(docs)],
        compiler_params=params,
        cost_estimate=cost(docs * pages.shape[1]),
    )(plan, kept, pages, partials[0])

    return pl.pallas_call(
        functools.partial(scores_kernel, (own, far, rest)),
        out_shape=jax.ShapeDtypeStruct((docs, total), jnp.float32),
        in_specs=[SMEM] + [VMEM] * (SPILL + 5),
        out_specs=VMEM,
        scratch_shapes=[pltpu.VMEM((2, 16, total // 2), jnp.float32)],
        compiler_params=params,
    )(plan, row, chosen, own_out[0], far_out[0], rest_home, *received)


def solution(mesh):
    split = Mesh(mesh.devices.reshape(SIZES), AXES)
    return jax.shard_map(
        local,
        mesh=split,
        in_specs=(P(AXES, None, None), P(), P(AXES, None, None), P(AXES), P(AXES), P(AXES)),
        out_specs=P(AXES, None),
        check_vma=False,
    )
```

```python
import functools

import jax
import jax.numpy as jnp
from jax import lax
from jax.experimental import pallas as pl
from jax.experimental.pallas import tpu as pltpu
from jax.sharding import Mesh, PartitionSpec as P

SPILL = 3
SIZES = (2, 4, 2, 8, 2)
AXES = ("xh", "y", "xl", "z", "c")
NX, NY, NZ, NC = 4, 4, 8, 2
CHUNK = NY * NZ
TILE = 256
WIDE = 2 * TILE
lowest = -1e30
VMEM_LIMIT = 48 * 1024 * 1024
TRANSPOSED = (((1,), (1,)), ((), ()))


def device_id(x, y, z, c):
    return (((x // 2) * NY + y) * 2 + x % 2) * NZ * NC + z * NC + c


def coordinates():
    return [
        (x, y, z, c) for x in range(NX) for y in range(NY) for z in range(NZ) for c in range(NC)
    ]


def along_x(value, steps):
    pairs = [
        (device_id(x, y, z, c), device_id((x + steps) % NX, y, z, c)) for x, y, z, c in coordinates()
    ]
    return lax.ppermute(value, AXES, pairs)


def other_core(value):
    pairs = [(device_id(x, y, z, c), device_id(x, y, z, 1 - c)) for x, y, z, c in coordinates()]
    return lax.ppermute(value, AXES, pairs)


def along_blk(value, steps):
    count = 32
    pairs = [
        (g * count + b, g * count + (b + steps) % count) for g in range(8) for b in range(count)
    ]
    return lax.ppermute(value, AXES, pairs)


def region_of(x_abs, core):
    return (x_abs // 2) * (NY * 2 * NZ * NC) + (x_abs % 2) * (NZ * NC) + core


PLACES = [y * (2 * NZ * NC) + z * NC for y in range(NY) for z in range(NZ)]


def chunk_total(len_ref, x_abs, core):
    first = region_of(x_abs, core)
    terms = [len_ref[first + place] for place in PLACES]
    while len(terms) > 1:
        terms = [sum(terms[i : i + 2]) for i in range(0, len(terms), 2)]
    return terms[0]


def chunk_of(spec, x, c):
    steps, core = spec
    return lax.rem(x + NX - steps, NX), (c if core == 0 else 1 - c)


def compact(len_ref, live_ref, base, chunk, source):
    tokens = source.shape[1]
    first = region_of(*chunk)
    at = base
    for k, place in enumerate(PLACES):
        live_ref[pl.ds(at, tokens), :] = source[k].astype(jnp.float32)
        at = at + len_ref[first + place]
    return at - base


def slot_ids(count_ref, offset_ref, helper_ref, pages):
    docs = count_ref.shape[0]
    ids = []
    for k in pages:
        slot = jnp.int32(0) if helper_ref is None else helper_ref[k]
        for j in range(docs):
            inside = (offset_ref[j] <= k) & (k < offset_ref[j] + count_ref[j])
            slot = jnp.where(inside, j, slot)
        ids.append(jnp.clip(slot, 0, (SPILL + 1) * docs - 1))
    return ids


def fill_tails(pages_ref, tail_ref):
    pages, patches, _ = pages_ref.shape
    whole = patches // 16 * 16
    tail_ref[...] = jnp.zeros(tail_ref.shape, jnp.float32)
    for p in range(pages):
        tail_ref[8 * p : 8 * p + patches - whole, :] = pages_ref[p, whole:, :].astype(jnp.float32)
        for extra in range(patches - whole, 8):
            tail_ref[8 * p + extra : 8 * p + extra + 1, :] = pages_ref[
                p, patches - 1 : patches, :
            ].astype(jnp.float32)
    return tail_ref[...].astype(jnp.bfloat16)


def page_best(token_rows, pages_ref, tails):
    pages, patches, _ = pages_ref.shape
    whole = patches // 16 * 16
    columns = token_rows.shape[0]
    tail_scores = lax.dot_general(
        tails, token_rows, TRANSPOSED, preferred_element_type=jnp.float32
    )
    rows = []
    for p in range(pages):
        scores = lax.dot_general(
            pages_ref[p, :whole, :], token_rows, TRANSPOSED, preferred_element_type=jnp.float32
        )
        best = jnp.max(scores.reshape(whole // 8, 8, columns), axis=0)
        best = jnp.maximum(best, tail_scores[8 * p : 8 * p + 8])
        rows.append(jnp.max(best, axis=0, keepdims=True))
    return rows


def over_tiles(total, visit):
    tiles = (total + TILE - 1) // TILE

    def four(i, _):
        visit(pl.multiple_of(i * (4 * TILE), 4 * TILE), 4 * TILE)
        return 0

    lax.fori_loop(0, tiles // 4, four, 0)
    done = tiles // 4 * 4

    @pl.when(tiles % 4 >= 2)
    def _():
        visit(pl.multiple_of(done * TILE, 4 * TILE), 2 * TILE)

    @pl.when(tiles % 2 == 1)
    def _():
        visit(pl.multiple_of((tiles - 1) * TILE, TILE), TILE)


def from_column(table_ref, first, span):
    if isinstance(first, int):
        return table_ref[:, first : first + span]
    lanes = 128
    base = pl.multiple_of(first // lanes * lanes, lanes)
    window = table_ref[:, pl.ds(base, span + lanes)]
    return pltpu.roll(window, lax.rem(span + lanes - (first - base), span + lanes), 1)[:, :span]


def own_position():
    return lax.axis_index("xh") * 2 + lax.axis_index("xl"), lax.axis_index("c")


def over_chunks(count, total_of, span, visit):
    def each(i, _):
        def tile(k, _):
            visit(i, pl.multiple_of(jnp.minimum(k * WIDE, span - WIDE), TILE))
            return 0

        lax.fori_loop(0, (total_of(i) + WIDE - 1) // WIDE, tile, 0)
        return 0

    lax.fori_loop(0, count, each, 0)


def whole_chunks(specs, plan_ref, sources, outs, pages_ref, live_ref, slot_ref, note_ref, ids, tails):
    x, c = own_position()
    room = live_ref.shape[0] // len(specs)
    for i, (spec, source) in enumerate(zip(specs, sources)):
        note_ref[i] = compact(plan_ref, live_ref, i * room, chunk_of(spec, x, c), source)

    docs, span = outs[0].shape[1:]

    def visit(i, at):
        base = pl.multiple_of(i * room, TILE)
        token_rows = live_ref[pl.ds(base + at, WIDE), :].astype(jnp.bfloat16)
        slot_ref[...] = jnp.full(slot_ref.shape, lowest, jnp.float32)
        for slot, best in zip(ids, page_best(token_rows, pages_ref, tails)):
            row = pl.ds(slot, 1)
            slot_ref[row, :] = jnp.maximum(slot_ref[row, :], best)
        for distance in range(SPILL + 1):
            outs[distance][i, :, pl.ds(at, WIDE)] = slot_ref[
                distance * docs : (distance + 1) * docs, :
            ]

    over_chunks(len(specs), lambda i: note_ref[i], span, visit)


def first_kernel(specs, len_hbm, count_hbm, offset_hbm, helper_hbm, *rest):
    sources, rest = rest[: len(specs)], rest[len(specs) :]
    pages_ref, rest = rest[0], rest[1:]
    outs, rest = rest[: SPILL + 1], rest[SPILL + 1 :]
    plan_ref, count_ref, offset_ref, helper_ref, live_ref, tail_ref, slot_ref, note_ref, sem = rest
    pages = pages_ref.shape[0]
    moves = [
        pltpu.make_async_copy(source, target, sem.at[i])
        for i, (source, target) in enumerate(
            (
                (len_hbm, plan_ref.at[pl.ds(0, len_hbm.shape[0])]),
                (count_hbm, count_ref),
                (offset_hbm, offset_ref),
                (helper_hbm, helper_ref),
            )
        )
    ]
    for move in moves:
        move.start()
    tails = fill_tails(pages_ref, tail_ref)
    for move in moves:
        move.wait()
    ids = slot_ids(count_ref, offset_ref, helper_ref, range(pages))
    at = len_hbm.shape[0]
    for k in range(pages):
        plan_ref[at + k] = ids[k]
    for chunk in range(NX * NC):
        plan_ref[at + pages + chunk] = chunk_total(plan_ref, chunk // NC, chunk % NC)
    whole_chunks(specs, plan_ref, sources, outs, pages_ref, live_ref, slot_ref, note_ref, ids, tails)


def more_kernel(specs, queries, plan_ref, *rest):
    sources, rest = rest[: len(specs)], rest[len(specs) :]
    pages_ref, rest = rest[0], rest[1:]
    outs, rest = rest[: SPILL + 1], rest[SPILL + 1 :]
    live_ref, tail_ref, slot_ref, note_ref = rest
    ids = [plan_ref[queries + k] for k in range(pages_ref.shape[0])]
    tails = fill_tails(pages_ref, tail_ref)
    whole_chunks(specs, plan_ref, sources, outs, pages_ref, live_ref, slot_ref, note_ref, ids, tails)


def chunk_count(plan_ref, chunk):
    return plan_ref[plan_ref.shape[0] - NX * NC + chunk[0] * NC + chunk[1]]


def most_tokens(plan_ref):
    most = plan_ref[plan_ref.shape[0] - NX * NC]
    for chunk in range(1, NX * NC):
        most = jnp.maximum(most, plan_ref[plan_ref.shape[0] - NX * NC + chunk])
    return most


def chosen_kernel(plan_ref, lens_ref, chosen_ref):
    span = chosen_ref.shape[0] // (NX * NC)
    half = chosen_ref.shape[1]
    starts, ends = query_columns(lens_ref[...], span)

    def step(tile, _):
        for chunk in range(NX * NC):
            lanes = slice(chunk // (2 * NC) * half, (chunk // (2 * NC) + 1) * half)
            first = pl.multiple_of(chunk * span + tile * TILE, TILE)
            token = lax.broadcasted_iota(jnp.int32, (TILE, half), 0) + first
            inside = (token >= starts[:, lanes]) & (token < ends[:, lanes])
            chosen_ref[pl.ds(first, TILE), :] = jnp.where(inside, 1.0, 0.0).astype(jnp.bfloat16)
        return 0

    lax.fori_loop(0, (most_tokens(plan_ref) + TILE - 1) // TILE, step, 0)


def query_columns(lens, span):
    queries = lens.shape[1]

    def chunk(n):
        return ((n // (NC * NZ * 2 * NY)) * 2 + (n // (NC * NZ)) % 2) * NC + n % NC

    def place(n):
        return (n // (NC * NZ * 2)) % NY * NZ + (n // NC) % NZ

    one = lax.broadcasted_iota(jnp.int32, (queries, queries), 0)
    two = lax.broadcasted_iota(jnp.int32, (queries, queries), 1)
    before = (chunk(one) == chunk(two)) & (place(one) < place(two))
    row = jnp.broadcast_to(lens.astype(jnp.float32).astype(jnp.bfloat16), (16, queries))
    starts = jnp.dot(
        row,
        jnp.where(before, 1.0, 0.0).astype(jnp.bfloat16),
        preferred_element_type=jnp.float32,
    )[0:1].astype(jnp.int32)
    starts = starts + chunk(lax.broadcasted_iota(jnp.int32, (1, queries), 1)) * span
    return starts, starts + lens


def late_kernel(specs, placed, queries, plan_ref, nothing_ref, *rest):
    sources, rest = rest[: len(specs)], rest[len(specs) :]
    all_pages_ref, rest = rest[0], rest[1:]
    before, rest = rest[: len(placed) * (SPILL + 1)], rest[len(placed) * (SPILL + 1) :]
    outs, rest = rest[: SPILL + 1], rest[SPILL + 1 :]
    kept_ref, live_ref, tail_ref, table_ref = rest
    docs, columns_all = outs[0].shape
    pages = all_pages_ref.shape[0]
    pages_ref = all_pages_ref.at[pl.ds(docs, pages - docs)]
    x, c = own_position()
    span = columns_all // (NX * NC)

    def column(spec):
        chunk = chunk_of(spec, x, c)
        return pl.multiple_of((chunk[0] * NC + chunk[1]) * span, TILE)

    for group, group_specs in enumerate(placed):
        for i, spec in enumerate(group_specs):
            for distance in range(SPILL + 1):
                outs[distance][:, pl.ds(column(spec), span)] = before[
                    group * (SPILL + 1) + distance
                ][i]
    ids = [plan_ref[queries + k] for k in range(docs, pages)]
    tails = fill_tails(pages_ref, tail_ref)
    firsts = [0]
    for spec, source in zip(specs, sources):
        chunk = chunk_of(spec, x, c)
        compact(plan_ref, live_ref, firsts[-1], chunk, source)
        firsts.append(firsts[-1] + chunk_count(plan_ref, chunk))

    nothing = nothing_ref[0:1, 0:1]

    def visit(at, size):
        token_rows = live_ref[pl.ds(at, size), :].astype(jnp.bfloat16)
        kept_ref[pl.ds(at, size), :] = token_rows
        here = pl.ds(at, size)
        table_ref[:, here] = jnp.broadcast_to(nothing, (table_ref.shape[0], size))
        for slot, best in zip(ids, page_best(token_rows, pages_ref, tails)):
            row = pl.ds(slot, 1)
            table_ref[row, here] = jnp.maximum(table_ref[row, here], best)

    over_tiles(firsts[-1], visit)
    for spec, first in zip(specs, firsts):
        value = from_column(table_ref, first, span)
        to = column(spec)
        for distance in range(SPILL + 1):
            outs[distance][:, pl.ds(to, span)] = value[distance * docs : (distance + 1) * docs]


def home_kernel(
    specs, queries, plan_ref, kept_ref, all_pages_ref, before_ref, out_ref, tail_ref, table_ref
):
    docs, span = out_ref.shape[1:]
    pages_ref = all_pages_ref.at[pl.ds(0, docs)]
    x, c = own_position()
    ids = [plan_ref[queries + k] for k in range(docs)]
    tails = fill_tails(pages_ref, tail_ref)
    chunks = [chunk_of(spec, x, c) for spec in specs]
    firsts = [0]
    for chunk in chunks:
        firsts.append(firsts[-1] + chunk_count(plan_ref, chunk))

    def visit(at, size):
        here = pl.ds(at, size)
        table_ref[:, here] = jnp.full((table_ref.shape[0], size), lowest, jnp.float32)
        for slot, best in zip(ids, page_best(kept_ref[here, :], pages_ref, tails)):
            row = pl.ds(slot, 1)
            table_ref[row, here] = jnp.maximum(table_ref[row, here], best)

    over_tiles(firsts[-1], visit)
    for i, (chunk, first) in enumerate(zip(chunks, firsts)):
        value = from_column(table_ref, first, span)
        to = pl.multiple_of((chunk[0] * NC + chunk[1]) * span, TILE)
        out_ref[i] = jnp.maximum(before_ref[:, pl.ds(to, span)], value[:docs])


def scores_kernel(groups, plan_ref, lens_ref, chosen_ref, *rest):
    homes, rest = rest[: len(groups)], rest[len(groups) :]
    received, (out_ref, acc_ref) = rest[:SPILL], rest[SPILL:]
    docs, columns_all = received[0].shape
    lens = lens_ref[...]
    span = columns_all // (NX * NC)
    x, c = own_position()
    acc_ref[...] = jnp.zeros(acc_ref.shape, jnp.float32)
    parts_list = [
        (home, i, chunk_of(spec, x, c))
        for home, group in zip(homes, groups)
        for i, spec in enumerate(group)
    ]

    def visit(at, size):
        added = []
        for home_ref, i, chunk in parts_list:
            to = pl.multiple_of((chunk[0] * NC + chunk[1]) * span + at, TILE)
            live = lax.broadcasted_iota(jnp.int32, (docs, size), 1) + at < chunk_count(
                plan_ref, chunk
            )
            value = home_ref[i, :, pl.ds(at, size)]
            for ref in received:
                value = jnp.maximum(value, ref[:, pl.ds(to, size)])
            value = jnp.where(live, value, 0.0)
            value = jnp.concatenate([value, jnp.zeros((8 - docs, size), jnp.float32)], axis=0)
            high = value.astype(jnp.bfloat16).astype(jnp.float32)
            left = value - high
            middle = left.astype(jnp.bfloat16).astype(jnp.float32)
            pieces = [high, middle, left - middle, jnp.zeros((8, size), jnp.float32)]
            left_side = jnp.concatenate(pieces, axis=0).astype(jnp.bfloat16)
            added.append(
                jnp.dot(
                    left_side, chosen_ref[pl.ds(to, size), :], preferred_element_type=jnp.float32
                )
            )
        for (_, _, chunk), value in zip(parts_list, added):
            acc_ref[chunk[0] // 2] = acc_ref[chunk[0] // 2] + value

    tiles = (most_tokens(plan_ref) + TILE - 1) // TILE

    @pl.when(tiles >= 2)
    def _():
        visit(0, 2 * TILE)

    @pl.when(tiles % 2 == 1)
    def _():
        visit(pl.multiple_of((tiles - 1) * TILE, TILE), TILE)

    half = acc_ref.shape[2]
    for x_hi in range(acc_ref.shape[0]):
        lanes = slice(x_hi * half, (x_hi + 1) * half)
        divisor = lens[:, lanes].astype(jnp.float32)
        high, middle, low = (acc_ref[x_hi, 8 * i : 8 * i + docs, :] for i in range(3))
        out_ref[:, lanes] = ((high + middle) + low) / divisor


SMEM = pl.BlockSpec(memory_space=pltpu.SMEM)
VMEM = pl.BlockSpec(memory_space=pltpu.VMEM)
HBM = pl.BlockSpec(memory_space=pltpu.HBM)


def lowest_kernel(out_ref):
    out_ref[...] = jnp.full(out_ref.shape, lowest, jnp.float32)


def local(queries, query_len, pages, page_count, page_offset, helper_doc):
    docs = page_count.shape[0]
    total = query_len.shape[0]
    tokens, width = queries.shape[1:]
    columns = total * tokens
    span = columns // (NX * NC)
    room = span + TILE
    params = pltpu.CompilerParams(vmem_limit_bytes=VMEM_LIMIT)
    whole = [jax.ShapeDtypeStruct((docs, columns), jnp.float32)] * (SPILL + 1)
    slots = pltpu.VMEM((16, WIDE), jnp.float32)
    notes = pltpu.SMEM((16,), jnp.int32)
    row = query_len[None, :]
    own, far, rest = [(0, 0), (0, 1)], [(2, 0)], [(2, 1), (1, 0), (1, 1), (3, 0), (3, 1)]
    pool = len(rest) * span + 2 * WIDE

    def part(specs):
        return [jax.ShapeDtypeStruct((len(specs), docs, span), jnp.float32)] * (SPILL + 1)

    def tail_room(count):
        return pltpu.VMEM((8 * count + 8 * count % 16, width), jnp.float32)

    def live_room(specs):
        return pltpu.VMEM((len(specs) * room, width), jnp.float32)

    def cost(rows):
        return pl.CostEstimate(
            flops=2 * rows * columns * width, bytes_accessed=rows * width * 2, transcendentals=0
        )

    nothing = pl.pallas_call(
        lowest_kernel,
        out_shape=jax.ShapeDtypeStruct((8, 128), jnp.float32),
        out_specs=VMEM,
        cost_estimate=cost(pages.shape[0] * pages.shape[1]),
    )()
    queries, nothing = lax.optimization_barrier((queries, nothing))
    copies = jnp.broadcast_to(queries, (CHUNK, tokens, width))
    mine = lax.all_to_all(copies, ("y", "z"), 0, 0, tiled=True)
    mine_other = other_core(mine)
    two, one, three = [along_x(mine, steps) for steps in (2, 1, 3)]

    *own_out, plan = pl.pallas_call(
        functools.partial(first_kernel, own),
        out_shape=part(own)
        + [jax.ShapeDtypeStruct((total + pages.shape[0] + NX * NC,), jnp.int32)],
        in_specs=[HBM] * 4 + [VMEM] * (len(own) + 1),
        out_specs=[VMEM] * (SPILL + 1) + [SMEM],
        scratch_shapes=[
            pltpu.SMEM(page_count.shape, jnp.int32),
            pltpu.SMEM(page_offset.shape, jnp.int32),
            pltpu.SMEM(helper_doc.shape, jnp.int32),
            live_room(own),
            tail_room(pages.shape[0]),
            slots,
            notes,
            pltpu.SemaphoreType.DMA((4,)),
        ],
        compiler_params=params,
        cost_estimate=cost(700),
    )(query_len, page_count, page_offset, helper_doc, mine, mine_other, pages)

    two, plan = lax.optimization_barrier((two, plan))
    far_out = pl.pallas_call(
        functools.partial(more_kernel, far, total),
        out_shape=part(far),
        in_specs=[SMEM] + [VMEM] * (len(far) + 1),
        out_specs=[VMEM] * (SPILL + 1),
        scratch_shapes=[live_room(far), tail_room(pages.shape[0]), slots, notes],
        compiler_params=params,
        cost_estimate=cost(700),
    )(plan, two, pages)

    one, two, three, far_out = lax.optimization_barrier((one, two, three, far_out))
    two_other, one_other, three_other = [other_core(value) for value in (two, one, three)]
    chosen = pl.pallas_call(
        chosen_kernel,
        out_shape=jax.ShapeDtypeStruct((columns, total // 2), jnp.bfloat16),
        in_specs=[SMEM, VMEM],
        out_specs=VMEM,
        compiler_params=params,
        cost_estimate=cost(pages.shape[1]),
    )(plan, row)
    arrived = [two_other, one, one_other, three, three_other]
    *arrived, chosen = lax.optimization_barrier((*arrived, chosen))

    *partials, kept = pl.pallas_call(
        functools.partial(late_kernel, rest, (own, far), total),
        out_shape=whole + [jax.ShapeDtypeStruct((pool, width), jnp.bfloat16)],
        in_specs=[SMEM] + [VMEM] * (len(rest) + 2 + 2 * (SPILL + 1)),
        out_specs=[VMEM] * (SPILL + 2),
        scratch_shapes=[
            pltpu.VMEM((pool, width), jnp.float32),
            tail_room(pages.shape[0] - docs),
            pltpu.VMEM((16, pool), jnp.float32),
        ],
        compiler_params=params,
        cost_estimate=cost((pages.shape[0] - docs) * pages.shape[1]),
    )(plan, nothing, *arrived, pages, *own_out, *far_out)
    received = [along_blk(partials[distance], -distance) for distance in range(1, SPILL + 1)]

    rest_home = pl.pallas_call(
        functools.partial(home_kernel, rest, total),
        out_shape=part(rest)[0],
        in_specs=[SMEM] + [VMEM] * 3,
        out_specs=VMEM,
        scratch_shapes=[tail_room(docs), pltpu.VMEM((8, pool), jnp.float32)],
        compiler_params=params,
        cost_estimate=cost(docs * pages.shape[1]),
    )(plan, kept, pages, partials[0])

    return pl.pallas_call(
        functools.partial(scores_kernel, (own, far, rest)),
        out_shape=jax.ShapeDtypeStruct((docs, total), jnp.float32),
        in_specs=[SMEM] + [VMEM] * (SPILL + 5),
        out_specs=VMEM,
        scratch_shapes=[pltpu.VMEM((2, 32, total // 2), jnp.float32)],
        compiler_params=params,
    )(plan, row, chosen, own_out[0], far_out[0], rest_home, *received)


def solution(mesh):
    split = Mesh(mesh.devices.reshape(SIZES), AXES)
    return jax.shard_map(
        local,
        mesh=split,
        in_specs=(P(AXES, None, None), P(), P(AXES, None, None), P(AXES), P(AXES), P(AXES)),
        out_specs=P(AXES, None),
        check_vma=False,
    )
```

```python
import functools

import jax
import jax.numpy as jnp
from jax import lax
from jax.experimental import pallas as pl
from jax.experimental.pallas import tpu as pltpu
from jax.sharding import Mesh, PartitionSpec as P

SPILL = 3
SEND_ORDER = (3, 1, 2)
SIZES = (2, 4, 2, 8, 2)
AXES = ("xh", "y", "xl", "z", "c")
NX, NY, NZ, NC = 4, 4, 8, 2
CHUNK = NY * NZ
TILE = 256
WIDE = 2 * TILE
lowest = -1e30
VMEM_LIMIT = 48 * 1024 * 1024
TRANSPOSED = (((1,), (1,)), ((), ()))


def device_id(x, y, z, c):
    return (((x // 2) * NY + y) * 2 + x % 2) * NZ * NC + z * NC + c


def coordinates():
    return [
        (x, y, z, c) for x in range(NX) for y in range(NY) for z in range(NZ) for c in range(NC)
    ]


def along_x(value, steps):
    pairs = [
        (device_id(x, y, z, c), device_id((x + steps) % NX, y, z, c)) for x, y, z, c in coordinates()
    ]
    return lax.ppermute(value, AXES, pairs)


def other_core(value):
    pairs = [(device_id(x, y, z, c), device_id(x, y, z, 1 - c)) for x, y, z, c in coordinates()]
    return lax.ppermute(value, AXES, pairs)


def along_blk(value, steps):
    count = 32
    pairs = [
        (g * count + b, g * count + (b + steps) % count) for g in range(8) for b in range(count)
    ]
    return lax.ppermute(value, AXES, pairs)


def region_of(x_abs, core):
    return (x_abs // 2) * (NY * 2 * NZ * NC) + (x_abs % 2) * (NZ * NC) + core


PLACES = [y * (2 * NZ * NC) + z * NC for y in range(NY) for z in range(NZ)]


def chunk_total(len_ref, x_abs, core):
    first = region_of(x_abs, core)
    terms = [len_ref[first + place] for place in PLACES]
    while len(terms) > 1:
        terms = [sum(terms[i : i + 2]) for i in range(0, len(terms), 2)]
    return terms[0]


def chunk_of(spec, x, c):
    steps, core = spec
    return lax.rem(x + NX - steps, NX), (c if core == 0 else 1 - c)


def compact(len_ref, live_ref, base, chunk, source):
    tokens = source.shape[1]
    first = region_of(*chunk)
    at = base
    for k, place in enumerate(PLACES):
        live_ref[pl.ds(at, tokens), :] = source[k].astype(jnp.float32)
        at = at + len_ref[first + place]
    return at - base


def slot_ids(count_ref, offset_ref, helper_ref, pages):
    docs = count_ref.shape[0]
    ids = []
    for k in pages:
        slot = jnp.int32(0) if helper_ref is None else helper_ref[k]
        for j in range(docs):
            inside = (offset_ref[j] <= k) & (k < offset_ref[j] + count_ref[j])
            slot = jnp.where(inside, j, slot)
        ids.append(jnp.clip(slot, 0, (SPILL + 1) * docs - 1))
    return ids


def fill_tails(pages_ref, tail_ref):
    pages, patches, _ = pages_ref.shape
    whole = patches // 16 * 16
    tail_ref[...] = jnp.zeros(tail_ref.shape, jnp.float32)
    for p in range(pages):
        tail_ref[8 * p : 8 * p + patches - whole, :] = pages_ref[p, whole:, :].astype(jnp.float32)
        for extra in range(patches - whole, 8):
            tail_ref[8 * p + extra : 8 * p + extra + 1, :] = pages_ref[
                p, patches - 1 : patches, :
            ].astype(jnp.float32)
    return tail_ref[...].astype(jnp.bfloat16)


def page_best(token_rows, pages_ref, tails):
    pages, patches, _ = pages_ref.shape
    whole = patches // 16 * 16
    columns = token_rows.shape[0]
    tail_scores = lax.dot_general(
        tails, token_rows, TRANSPOSED, preferred_element_type=jnp.float32
    )
    rows = []
    for p in range(pages):
        scores = lax.dot_general(
            pages_ref[p, :whole, :], token_rows, TRANSPOSED, preferred_element_type=jnp.float32
        )
        best = jnp.max(scores.reshape(whole // 8, 8, columns), axis=0)
        best = jnp.maximum(best, tail_scores[8 * p : 8 * p + 8])
        rows.append(jnp.max(best, axis=0, keepdims=True))
    return rows


def over_tiles(total, visit):
    tiles = (total + TILE - 1) // TILE

    def four(i, _):
        visit(pl.multiple_of(i * (4 * TILE), 4 * TILE), 4 * TILE)
        return 0

    lax.fori_loop(0, tiles // 4, four, 0)
    done = tiles // 4 * 4

    @pl.when(tiles % 4 >= 2)
    def _():
        visit(pl.multiple_of(done * TILE, 4 * TILE), 2 * TILE)

    @pl.when(tiles % 2 == 1)
    def _():
        visit(pl.multiple_of((tiles - 1) * TILE, TILE), TILE)


def from_column(table_ref, first, span):
    if isinstance(first, int):
        return table_ref[:, first : first + span]
    lanes = 128
    base = pl.multiple_of(first // lanes * lanes, lanes)
    window = table_ref[:, pl.ds(base, span + lanes)]
    return pltpu.roll(window, lax.rem(span + lanes - (first - base), span + lanes), 1)[:, :span]


def own_position():
    return lax.axis_index("xh") * 2 + lax.axis_index("xl"), lax.axis_index("c")


def over_chunks(count, total_of, span, visit):
    def each(i, _):
        def tile(k, _):
            visit(i, pl.multiple_of(jnp.minimum(k * WIDE, span - WIDE), TILE))
            return 0

        lax.fori_loop(0, (total_of(i) + WIDE - 1) // WIDE, tile, 0)
        return 0

    lax.fori_loop(0, count, each, 0)


def whole_chunks(specs, plan_ref, sources, outs, pages_ref, live_ref, slot_ref, note_ref, ids, tails):
    x, c = own_position()
    room = live_ref.shape[0] // len(specs)
    for i, (spec, source) in enumerate(zip(specs, sources)):
        note_ref[i] = compact(plan_ref, live_ref, i * room, chunk_of(spec, x, c), source)

    docs, span = outs[0].shape[1:]

    def visit(i, at):
        base = pl.multiple_of(i * room, TILE)
        token_rows = live_ref[pl.ds(base + at, WIDE), :].astype(jnp.bfloat16)
        slot_ref[...] = jnp.full(slot_ref.shape, lowest, jnp.float32)
        for slot, best in zip(ids, page_best(token_rows, pages_ref, tails)):
            row = pl.ds(slot, 1)
            slot_ref[row, :] = jnp.maximum(slot_ref[row, :], best)
        for distance in range(SPILL + 1):
            outs[distance][i, :, pl.ds(at, WIDE)] = slot_ref[
                distance * docs : (distance + 1) * docs, :
            ]

    over_chunks(len(specs), lambda i: note_ref[i], span, visit)


def first_kernel(specs, len_hbm, count_hbm, offset_hbm, helper_hbm, *rest):
    sources, rest = rest[: len(specs)], rest[len(specs) :]
    pages_ref, rest = rest[0], rest[1:]
    outs, rest = rest[: SPILL + 1], rest[SPILL + 1 :]
    plan_ref, count_ref, offset_ref, helper_ref, live_ref, tail_ref, slot_ref, note_ref, sem = rest
    pages = pages_ref.shape[0]
    moves = [
        pltpu.make_async_copy(source, target, sem.at[i])
        for i, (source, target) in enumerate(
            (
                (len_hbm, plan_ref.at[pl.ds(0, len_hbm.shape[0])]),
                (count_hbm, count_ref),
                (offset_hbm, offset_ref),
                (helper_hbm, helper_ref),
            )
        )
    ]
    for move in moves:
        move.start()
    tails = fill_tails(pages_ref, tail_ref)
    for move in moves:
        move.wait()
    ids = slot_ids(count_ref, offset_ref, helper_ref, range(pages))
    at = len_hbm.shape[0]
    for k in range(pages):
        plan_ref[at + k] = ids[k]
    for chunk in range(NX * NC):
        plan_ref[at + pages + chunk] = chunk_total(plan_ref, chunk // NC, chunk % NC)
    whole_chunks(specs, plan_ref, sources, outs, pages_ref, live_ref, slot_ref, note_ref, ids, tails)


def more_kernel(specs, queries, plan_ref, *rest):
    sources, rest = rest[: len(specs)], rest[len(specs) :]
    pages_ref, rest = rest[0], rest[1:]
    outs, rest = rest[: SPILL + 1], rest[SPILL + 1 :]
    live_ref, tail_ref, slot_ref, note_ref = rest
    ids = [plan_ref[queries + k] for k in range(pages_ref.shape[0])]
    tails = fill_tails(pages_ref, tail_ref)
    whole_chunks(specs, plan_ref, sources, outs, pages_ref, live_ref, slot_ref, note_ref, ids, tails)


def chunk_count(plan_ref, chunk):
    return plan_ref[plan_ref.shape[0] - NX * NC + chunk[0] * NC + chunk[1]]


def most_tokens(plan_ref):
    most = plan_ref[plan_ref.shape[0] - NX * NC]
    for chunk in range(1, NX * NC):
        most = jnp.maximum(most, plan_ref[plan_ref.shape[0] - NX * NC + chunk])
    return most


def chosen_kernel(plan_ref, lens_ref, chosen_ref):
    span = chosen_ref.shape[0] // (NX * NC)
    half = chosen_ref.shape[1]
    starts, ends = query_columns(lens_ref[...], span)

    def step(tile, _):
        for chunk in range(NX * NC):
            lanes = slice(chunk // (2 * NC) * half, (chunk // (2 * NC) + 1) * half)
            first = pl.multiple_of(chunk * span + tile * TILE, TILE)
            token = lax.broadcasted_iota(jnp.int32, (TILE, half), 0) + first
            inside = (token >= starts[:, lanes]) & (token < ends[:, lanes])
            chosen_ref[pl.ds(first, TILE), :] = jnp.where(inside, 1.0, 0.0).astype(jnp.bfloat16)
        return 0

    lax.fori_loop(0, (most_tokens(plan_ref) + TILE - 1) // TILE, step, 0)


def query_columns(lens, span):
    queries = lens.shape[1]

    def chunk(n):
        return ((n // (NC * NZ * 2 * NY)) * 2 + (n // (NC * NZ)) % 2) * NC + n % NC

    def place(n):
        return (n // (NC * NZ * 2)) % NY * NZ + (n // NC) % NZ

    one = lax.broadcasted_iota(jnp.int32, (queries, queries), 0)
    two = lax.broadcasted_iota(jnp.int32, (queries, queries), 1)
    before = (chunk(one) == chunk(two)) & (place(one) < place(two))
    row = jnp.broadcast_to(lens.astype(jnp.float32).astype(jnp.bfloat16), (16, queries))
    starts = jnp.dot(
        row,
        jnp.where(before, 1.0, 0.0).astype(jnp.bfloat16),
        preferred_element_type=jnp.float32,
    )[0:1].astype(jnp.int32)
    starts = starts + chunk(lax.broadcasted_iota(jnp.int32, (1, queries), 1)) * span
    return starts, starts + lens


def late_kernel(specs, placed, queries, plan_ref, nothing_ref, *rest):
    sources, rest = rest[: len(specs)], rest[len(specs) :]
    all_pages_ref, rest = rest[0], rest[1:]
    before, rest = rest[: len(placed) * (SPILL + 1)], rest[len(placed) * (SPILL + 1) :]
    outs, rest = rest[: SPILL + 1], rest[SPILL + 1 :]
    kept_ref, live_ref, tail_ref, table_ref = rest
    docs, columns_all = outs[0].shape
    pages = all_pages_ref.shape[0]
    pages_ref = all_pages_ref.at[pl.ds(docs, pages - docs)]
    x, c = own_position()
    span = columns_all // (NX * NC)

    def column(spec):
        chunk = chunk_of(spec, x, c)
        return pl.multiple_of((chunk[0] * NC + chunk[1]) * span, TILE)

    for group, group_specs in enumerate(placed):
        for i, spec in enumerate(group_specs):
            for distance in range(SPILL + 1):
                outs[distance][:, pl.ds(column(spec), span)] = before[
                    group * (SPILL + 1) + distance
                ][i]
    ids = [plan_ref[queries + k] for k in range(docs, pages)]
    tails = fill_tails(pages_ref, tail_ref)
    firsts = [0]
    for spec, source in zip(specs, sources):
        chunk = chunk_of(spec, x, c)
        compact(plan_ref, live_ref, firsts[-1], chunk, source)
        firsts.append(firsts[-1] + chunk_count(plan_ref, chunk))

    nothing = nothing_ref[0:1, 0:1]

    def visit(at, size):
        token_rows = live_ref[pl.ds(at, size), :].astype(jnp.bfloat16)
        kept_ref[pl.ds(at, size), :] = token_rows
        here = pl.ds(at, size)
        table_ref[:, here] = jnp.broadcast_to(nothing, (table_ref.shape[0], size))
        for slot, best in zip(ids, page_best(token_rows, pages_ref, tails)):
            row = pl.ds(slot, 1)
            table_ref[row, here] = jnp.maximum(table_ref[row, here], best)

    over_tiles(firsts[-1], visit)
    for spec, first in zip(specs, firsts):
        value = from_column(table_ref, first, span)
        to = column(spec)
        for distance in range(SPILL + 1):
            outs[distance][:, pl.ds(to, span)] = value[distance * docs : (distance + 1) * docs]


def home_kernel(
    specs, queries, plan_ref, kept_ref, all_pages_ref, before_ref, out_ref, tail_ref, table_ref
):
    docs, span = out_ref.shape[1:]
    pages_ref = all_pages_ref.at[pl.ds(0, docs)]
    x, c = own_position()
    ids = [plan_ref[queries + k] for k in range(docs)]
    tails = fill_tails(pages_ref, tail_ref)
    chunks = [chunk_of(spec, x, c) for spec in specs]
    firsts = [0]
    for chunk in chunks:
        firsts.append(firsts[-1] + chunk_count(plan_ref, chunk))

    def visit(at, size):
        here = pl.ds(at, size)
        table_ref[:, here] = jnp.full((table_ref.shape[0], size), lowest, jnp.float32)
        for slot, best in zip(ids, page_best(kept_ref[here, :], pages_ref, tails)):
            row = pl.ds(slot, 1)
            table_ref[row, here] = jnp.maximum(table_ref[row, here], best)

    over_tiles(firsts[-1], visit)
    for i, (chunk, first) in enumerate(zip(chunks, firsts)):
        value = from_column(table_ref, first, span)
        to = pl.multiple_of((chunk[0] * NC + chunk[1]) * span, TILE)
        out_ref[i] = jnp.maximum(before_ref[:, pl.ds(to, span)], value[:docs])


def scores_kernel(groups, plan_ref, lens_ref, chosen_ref, *rest):
    homes, rest = rest[: len(groups)], rest[len(groups) :]
    received, (out_ref, acc_ref) = rest[:SPILL], rest[SPILL:]
    docs, columns_all = received[0].shape
    lens = lens_ref[...]
    span = columns_all // (NX * NC)
    x, c = own_position()
    acc_ref[...] = jnp.zeros(acc_ref.shape, jnp.float32)
    parts_list = [
        (home, i, chunk_of(spec, x, c))
        for home, group in zip(homes, groups)
        for i, spec in enumerate(group)
    ]

    def visit(at, size):
        added = []
        for home_ref, i, chunk in parts_list:
            to = pl.multiple_of((chunk[0] * NC + chunk[1]) * span + at, TILE)
            live = lax.broadcasted_iota(jnp.int32, (docs, size), 1) + at < chunk_count(
                plan_ref, chunk
            )
            value = home_ref[i, :, pl.ds(at, size)]
            for ref in received:
                value = jnp.maximum(value, ref[:, pl.ds(to, size)])
            value = jnp.where(live, value, 0.0)
            value = jnp.concatenate([value, jnp.zeros((8 - docs, size), jnp.float32)], axis=0)
            high = value.astype(jnp.bfloat16).astype(jnp.float32)
            left = value - high
            middle = left.astype(jnp.bfloat16).astype(jnp.float32)
            pieces = [high, middle, left - middle, jnp.zeros((8, size), jnp.float32)]
            left_side = jnp.concatenate(pieces, axis=0).astype(jnp.bfloat16)
            added.append(
                jnp.dot(
                    left_side, chosen_ref[pl.ds(to, size), :], preferred_element_type=jnp.float32
                )
            )
        for (_, _, chunk), value in zip(parts_list, added):
            acc_ref[chunk[0] // 2] = acc_ref[chunk[0] // 2] + value

    tiles = (most_tokens(plan_ref) + TILE - 1) // TILE

    @pl.when(tiles >= 2)
    def _():
        visit(0, 2 * TILE)

    @pl.when(tiles % 2 == 1)
    def _():
        visit(pl.multiple_of((tiles - 1) * TILE, TILE), TILE)

    half = acc_ref.shape[2]
    for x_hi in range(acc_ref.shape[0]):
        lanes = slice(x_hi * half, (x_hi + 1) * half)
        divisor = lens[:, lanes].astype(jnp.float32)
        high, middle, low = (acc_ref[x_hi, 8 * i : 8 * i + docs, :] for i in range(3))
        out_ref[:, lanes] = ((high + middle) + low) / divisor


SMEM = pl.BlockSpec(memory_space=pltpu.SMEM)
VMEM = pl.BlockSpec(memory_space=pltpu.VMEM)
HBM = pl.BlockSpec(memory_space=pltpu.HBM)


def lowest_kernel(out_ref):
    out_ref[...] = jnp.full(out_ref.shape, lowest, jnp.float32)


def local(queries, query_len, pages, page_count, page_offset, helper_doc):
    docs = page_count.shape[0]
    total = query_len.shape[0]
    tokens, width = queries.shape[1:]
    columns = total * tokens
    span = columns // (NX * NC)
    room = span + TILE
    params = pltpu.CompilerParams(vmem_limit_bytes=VMEM_LIMIT)
    whole = [jax.ShapeDtypeStruct((docs, columns), jnp.float32)] * (SPILL + 1)
    slots = pltpu.VMEM((16, WIDE), jnp.float32)
    notes = pltpu.SMEM((16,), jnp.int32)
    row = query_len[None, :]
    own, far, rest = [(0, 0), (0, 1)], [(2, 0)], [(2, 1), (1, 0), (1, 1), (3, 0), (3, 1)]
    pool = len(rest) * span + 2 * WIDE

    def part(specs):
        return [jax.ShapeDtypeStruct((len(specs), docs, span), jnp.float32)] * (SPILL + 1)

    def tail_room(count):
        return pltpu.VMEM((8 * count + 8 * count % 16, width), jnp.float32)

    def live_room(specs):
        return pltpu.VMEM((len(specs) * room, width), jnp.float32)

    def cost(rows):
        return pl.CostEstimate(
            flops=2 * rows * columns * width, bytes_accessed=rows * width * 2, transcendentals=0
        )

    nothing = pl.pallas_call(
        lowest_kernel,
        out_shape=jax.ShapeDtypeStruct((8, 128), jnp.float32),
        out_specs=VMEM,
        cost_estimate=cost(pages.shape[0] * pages.shape[1]),
    )()
    queries, nothing = lax.optimization_barrier((queries, nothing))
    copies = jnp.broadcast_to(queries, (CHUNK, tokens, width))
    mine = lax.all_to_all(copies, ("y", "z"), 0, 0, tiled=True)
    mine_other = other_core(mine)
    two, one, three = [along_x(mine, steps) for steps in (2, 1, 3)]

    *own_out, plan = pl.pallas_call(
        functools.partial(first_kernel, own),
        out_shape=part(own)
        + [jax.ShapeDtypeStruct((total + pages.shape[0] + NX * NC,), jnp.int32)],
        in_specs=[HBM] * 4 + [VMEM] * (len(own) + 1),
        out_specs=[VMEM] * (SPILL + 1) + [SMEM],
        scratch_shapes=[
            pltpu.SMEM(page_count.shape, jnp.int32),
            pltpu.SMEM(page_offset.shape, jnp.int32),
            pltpu.SMEM(helper_doc.shape, jnp.int32),
            live_room(own),
            tail_room(pages.shape[0]),
            slots,
            notes,
            pltpu.SemaphoreType.DMA((4,)),
        ],
        compiler_params=params,
        cost_estimate=cost(700),
    )(query_len, page_count, page_offset, helper_doc, mine, mine_other, pages)

    two, plan = lax.optimization_barrier((two, plan))
    far_out = pl.pallas_call(
        functools.partial(more_kernel, far, total),
        out_shape=part(far),
        in_specs=[SMEM] + [VMEM] * (len(far) + 1),
        out_specs=[VMEM] * (SPILL + 1),
        scratch_shapes=[live_room(far), tail_room(pages.shape[0]), slots, notes],
        compiler_params=params,
        cost_estimate=cost(700),
    )(plan, two, pages)

    one, two, three, far_out = lax.optimization_barrier((one, two, three, far_out))
    two_other, one_other, three_other = [other_core(value) for value in (two, one, three)]
    chosen = pl.pallas_call(
        chosen_kernel,
        out_shape=jax.ShapeDtypeStruct((columns, total // 2), jnp.bfloat16),
        in_specs=[SMEM, VMEM],
        out_specs=VMEM,
        compiler_params=params,
        cost_estimate=cost(pages.shape[1]),
    )(plan, row)
    arrived = [two_other, one, one_other, three, three_other]
    *arrived, chosen = lax.optimization_barrier((*arrived, chosen))

    *partials, kept = pl.pallas_call(
        functools.partial(late_kernel, rest, (own, far), total),
        out_shape=whole + [jax.ShapeDtypeStruct((pool, width), jnp.bfloat16)],
        in_specs=[SMEM] + [VMEM] * (len(rest) + 2 + 2 * (SPILL + 1)),
        out_specs=[VMEM] * (SPILL + 2),
        scratch_shapes=[
            pltpu.VMEM((pool, width), jnp.float32),
            tail_room(pages.shape[0] - docs),
            pltpu.VMEM((16, pool), jnp.float32),
        ],
        compiler_params=params,
        cost_estimate=cost((pages.shape[0] - docs) * pages.shape[1]),
    )(plan, nothing, *arrived, pages, *own_out, *far_out)
    received = [along_blk(partials[distance], -distance) for distance in SEND_ORDER]

    rest_home = pl.pallas_call(
        functools.partial(home_kernel, rest, total),
        out_shape=part(rest)[0],
        in_specs=[SMEM] + [VMEM] * 3,
        out_specs=VMEM,
        scratch_shapes=[tail_room(docs), pltpu.VMEM((8, pool), jnp.float32)],
        compiler_params=params,
        cost_estimate=cost(docs * pages.shape[1]),
    )(plan, kept, pages, partials[0])

    return pl.pallas_call(
        functools.partial(scores_kernel, (own, far, rest)),
        out_shape=jax.ShapeDtypeStruct((docs, total), jnp.float32),
        in_specs=[SMEM] + [VMEM] * (SPILL + 5),
        out_specs=VMEM,
        scratch_shapes=[pltpu.VMEM((2, 32, total // 2), jnp.float32)],
        compiler_params=params,
    )(plan, row, chosen, own_out[0], far_out[0], rest_home, *received)


def solution(mesh):
    split = Mesh(mesh.devices.reshape(SIZES), AXES)
    return jax.shard_map(
        local,
        mesh=split,
        in_specs=(P(AXES, None, None), P(), P(AXES, None, None), P(AXES), P(AXES), P(AXES)),
        out_specs=P(AXES, None),
        check_vma=False,
    )
```

```python
import functools

import jax
import jax.numpy as jnp
from jax import lax
from jax.experimental import pallas as pl
from jax.experimental.pallas import tpu as pltpu
from jax.sharding import Mesh, PartitionSpec as P

SPILL = 3
SEND_ORDER = (3, 1, 2)
SIZES = (2, 4, 2, 8, 2)
AXES = ("xh", "y", "xl", "z", "c")
NX, NY, NZ, NC = 4, 4, 8, 2
CHUNK = NY * NZ
TILE = 256
WIDE = 2 * TILE
lowest = -1e30
VMEM_LIMIT = 48 * 1024 * 1024
TRANSPOSED = (((1,), (1,)), ((), ()))


def device_id(x, y, z, c):
    return (((x // 2) * NY + y) * 2 + x % 2) * NZ * NC + z * NC + c


def coordinates():
    return [
        (x, y, z, c) for x in range(NX) for y in range(NY) for z in range(NZ) for c in range(NC)
    ]


def along_x(value, steps):
    pairs = [
        (device_id(x, y, z, c), device_id((x + steps) % NX, y, z, c)) for x, y, z, c in coordinates()
    ]
    return lax.ppermute(value, AXES, pairs)


def other_core(value):
    pairs = [(device_id(x, y, z, c), device_id(x, y, z, 1 - c)) for x, y, z, c in coordinates()]
    return lax.ppermute(value, AXES, pairs)


def along_blk(value, steps):
    count = 32
    pairs = [
        (g * count + b, g * count + (b + steps) % count) for g in range(8) for b in range(count)
    ]
    return lax.ppermute(value, AXES, pairs)


def region_of(x_abs, core):
    return (x_abs // 2) * (NY * 2 * NZ * NC) + (x_abs % 2) * (NZ * NC) + core


PLACES = [y * (2 * NZ * NC) + z * NC for y in range(NY) for z in range(NZ)]


def chunk_total(len_ref, x_abs, core):
    first = region_of(x_abs, core)
    terms = [len_ref[first + place] for place in PLACES]
    while len(terms) > 1:
        terms = [sum(terms[i : i + 2]) for i in range(0, len(terms), 2)]
    return terms[0]


def chunk_of(spec, x, c):
    steps, core = spec
    return lax.rem(x + NX - steps, NX), (c if core == 0 else 1 - c)


def compact(len_ref, live_ref, base, chunk, source):
    tokens = source.shape[1]
    first = region_of(*chunk)
    at = base
    for k, place in enumerate(PLACES):
        live_ref[pl.ds(at, tokens), :] = source[k].astype(jnp.float32)
        at = at + len_ref[first + place]
    return at - base


def slot_ids(count_ref, offset_ref, helper_ref, pages):
    docs = count_ref.shape[0]
    ids = []
    for k in pages:
        slot = jnp.int32(0) if helper_ref is None else helper_ref[k]
        for j in range(docs):
            inside = (offset_ref[j] <= k) & (k < offset_ref[j] + count_ref[j])
            slot = jnp.where(inside, j, slot)
        ids.append(jnp.clip(slot, 0, (SPILL + 1) * docs - 1))
    return ids


def fill_tails(pages_ref, tail_ref):
    pages, patches, _ = pages_ref.shape
    whole = patches // 16 * 16
    tail_ref[...] = jnp.zeros(tail_ref.shape, jnp.float32)
    for p in range(pages):
        tail_ref[8 * p : 8 * p + patches - whole, :] = pages_ref[p, whole:, :].astype(jnp.float32)
        for extra in range(patches - whole, 8):
            tail_ref[8 * p + extra : 8 * p + extra + 1, :] = pages_ref[
                p, patches - 1 : patches, :
            ].astype(jnp.float32)
    return tail_ref[...].astype(jnp.bfloat16)


def page_best(token_rows, pages_ref, tails):
    pages, patches, _ = pages_ref.shape
    whole = patches // 16 * 16
    columns = token_rows.shape[0]
    tail_scores = lax.dot_general(
        tails, token_rows, TRANSPOSED, preferred_element_type=jnp.float32
    )
    rows = []
    for p in range(pages):
        scores = lax.dot_general(
            pages_ref[p, :whole, :], token_rows, TRANSPOSED, preferred_element_type=jnp.float32
        )
        best = jnp.max(scores.reshape(whole // 8, 8, columns), axis=0)
        best = jnp.maximum(best, tail_scores[8 * p : 8 * p + 8])
        rows.append(jnp.max(best, axis=0, keepdims=True))
    return rows


def over_tiles(total, visit):
    tiles = (total + TILE - 1) // TILE

    def four(i, _):
        visit(pl.multiple_of(i * (4 * TILE), 4 * TILE), 4 * TILE)
        return 0

    lax.fori_loop(0, tiles // 4, four, 0)
    done = tiles // 4 * 4

    @pl.when(tiles % 4 >= 2)
    def _():
        visit(pl.multiple_of(done * TILE, 4 * TILE), 2 * TILE)

    @pl.when(tiles % 2 == 1)
    def _():
        visit(pl.multiple_of((tiles - 1) * TILE, TILE), TILE)


def from_column(table_ref, first, span):
    if isinstance(first, int):
        return table_ref[:, first : first + span]
    lanes = 128
    base = pl.multiple_of(first // lanes * lanes, lanes)
    window = table_ref[:, pl.ds(base, span + lanes)]
    return pltpu.roll(window, lax.rem(span + lanes - (first - base), span + lanes), 1)[:, :span]


def own_position():
    return lax.axis_index("xh") * 2 + lax.axis_index("xl"), lax.axis_index("c")


def over_chunks(count, total_of, span, visit):
    def each(i, _):
        def tile(k, _):
            visit(i, pl.multiple_of(jnp.minimum(k * WIDE, span - WIDE), TILE))
            return 0

        lax.fori_loop(0, (total_of(i) + WIDE - 1) // WIDE, tile, 0)
        return 0

    lax.fori_loop(0, count, each, 0)


def whole_chunks(specs, plan_ref, sources, outs, pages_ref, live_ref, slot_ref, note_ref, ids, tails):
    x, c = own_position()
    room = live_ref.shape[0] // len(specs)
    for i, (spec, source) in enumerate(zip(specs, sources)):
        note_ref[i] = compact(plan_ref, live_ref, i * room, chunk_of(spec, x, c), source)

    docs, span = outs[0].shape[1:]

    def visit(i, at):
        base = pl.multiple_of(i * room, TILE)
        token_rows = live_ref[pl.ds(base + at, WIDE), :].astype(jnp.bfloat16)
        slot_ref[...] = jnp.full(slot_ref.shape, lowest, jnp.float32)
        for slot, best in zip(ids, page_best(token_rows, pages_ref, tails)):
            row = pl.ds(slot, 1)
            slot_ref[row, :] = jnp.maximum(slot_ref[row, :], best)
        for distance in range(SPILL + 1):
            outs[distance][i, :, pl.ds(at, WIDE)] = slot_ref[
                distance * docs : (distance + 1) * docs, :
            ]

    over_chunks(len(specs), lambda i: note_ref[i], span, visit)


def first_kernel(specs, len_hbm, count_hbm, offset_hbm, helper_hbm, *rest):
    sources, rest = rest[: len(specs)], rest[len(specs) :]
    pages_ref, rest = rest[0], rest[1:]
    outs, rest = rest[: SPILL + 1], rest[SPILL + 1 :]
    plan_ref, count_ref, offset_ref, helper_ref, live_ref, tail_ref, slot_ref, note_ref, sem = rest
    pages = pages_ref.shape[0]
    moves = [
        pltpu.make_async_copy(source, target, sem.at[i])
        for i, (source, target) in enumerate(
            (
                (len_hbm, plan_ref.at[pl.ds(0, len_hbm.shape[0])]),
                (count_hbm, count_ref),
                (offset_hbm, offset_ref),
                (helper_hbm, helper_ref),
            )
        )
    ]
    for move in moves:
        move.start()
    tails = fill_tails(pages_ref, tail_ref)
    for move in moves:
        move.wait()
    ids = slot_ids(count_ref, offset_ref, helper_ref, range(pages))
    at = len_hbm.shape[0]
    for k in range(pages):
        plan_ref[at + k] = ids[k]
    for chunk in range(NX * NC):
        plan_ref[at + pages + chunk] = chunk_total(plan_ref, chunk // NC, chunk % NC)
    whole_chunks(specs, plan_ref, sources, outs, pages_ref, live_ref, slot_ref, note_ref, ids, tails)


def more_kernel(specs, queries, plan_ref, *rest):
    sources, rest = rest[: len(specs)], rest[len(specs) :]
    pages_ref, rest = rest[0], rest[1:]
    outs, rest = rest[: SPILL + 1], rest[SPILL + 1 :]
    live_ref, tail_ref, slot_ref, note_ref = rest
    ids = [plan_ref[queries + k] for k in range(pages_ref.shape[0])]
    tails = fill_tails(pages_ref, tail_ref)
    whole_chunks(specs, plan_ref, sources, outs, pages_ref, live_ref, slot_ref, note_ref, ids, tails)


def chunk_count(plan_ref, chunk):
    return plan_ref[plan_ref.shape[0] - NX * NC + chunk[0] * NC + chunk[1]]


def most_tokens(plan_ref):
    most = plan_ref[plan_ref.shape[0] - NX * NC]
    for chunk in range(1, NX * NC):
        most = jnp.maximum(most, plan_ref[plan_ref.shape[0] - NX * NC + chunk])
    return most


def chosen_kernel(plan_ref, lens_ref, chosen_ref):
    span = chosen_ref.shape[0] // (NX * NC)
    half = chosen_ref.shape[1]
    starts, ends = query_columns(lens_ref[...], span)

    def step(tile, _):
        for chunk in range(NX * NC):
            lanes = slice(chunk // (2 * NC) * half, (chunk // (2 * NC) + 1) * half)
            first = pl.multiple_of(chunk * span + tile * TILE, TILE)
            token = lax.broadcasted_iota(jnp.int32, (TILE, half), 0) + first
            inside = (token >= starts[:, lanes]) & (token < ends[:, lanes])
            chosen_ref[pl.ds(first, TILE), :] = jnp.where(inside, 1.0, 0.0).astype(jnp.bfloat16)
        return 0

    lax.fori_loop(0, (most_tokens(plan_ref) + TILE - 1) // TILE, step, 0)


def query_columns(lens, span):
    queries = lens.shape[1]

    def chunk(n):
        return ((n // (NC * NZ * 2 * NY)) * 2 + (n // (NC * NZ)) % 2) * NC + n % NC

    def place(n):
        return (n // (NC * NZ * 2)) % NY * NZ + (n // NC) % NZ

    one = lax.broadcasted_iota(jnp.int32, (queries, queries), 0)
    two = lax.broadcasted_iota(jnp.int32, (queries, queries), 1)
    before = (chunk(one) == chunk(two)) & (place(one) < place(two))
    row = jnp.broadcast_to(lens.astype(jnp.float32).astype(jnp.bfloat16), (16, queries))
    starts = jnp.dot(
        row,
        jnp.where(before, 1.0, 0.0).astype(jnp.bfloat16),
        preferred_element_type=jnp.float32,
    )[0:1].astype(jnp.int32)
    starts = starts + chunk(lax.broadcasted_iota(jnp.int32, (1, queries), 1)) * span
    return starts, starts + lens


def late_kernel(specs, placed, queries, plan_ref, nothing_ref, *rest):
    sources, rest = rest[: len(specs)], rest[len(specs) :]
    all_pages_ref, rest = rest[0], rest[1:]
    before, rest = rest[: len(placed) * (SPILL + 1)], rest[len(placed) * (SPILL + 1) :]
    outs, rest = rest[: SPILL + 1], rest[SPILL + 1 :]
    kept_ref, live_ref, tail_ref, table_ref = rest
    docs, columns_all = outs[0].shape
    pages = all_pages_ref.shape[0]
    pages_ref = all_pages_ref.at[pl.ds(docs, pages - docs)]
    x, c = own_position()
    span = columns_all // (NX * NC)

    def column(spec):
        chunk = chunk_of(spec, x, c)
        return pl.multiple_of((chunk[0] * NC + chunk[1]) * span, TILE)

    for group, group_specs in enumerate(placed):
        for i, spec in enumerate(group_specs):
            for distance in range(SPILL + 1):
                outs[distance][:, pl.ds(column(spec), span)] = before[
                    group * (SPILL + 1) + distance
                ][i]
    ids = [plan_ref[queries + k] for k in range(docs, pages)]
    tails = fill_tails(pages_ref, tail_ref)
    firsts = [0]
    for spec, source in zip(specs, sources):
        chunk = chunk_of(spec, x, c)
        compact(plan_ref, live_ref, firsts[-1], chunk, source)
        firsts.append(firsts[-1] + chunk_count(plan_ref, chunk))

    nothing = nothing_ref[0:1, 0:1]

    def visit(at, size):
        token_rows = live_ref[pl.ds(at, size), :].astype(jnp.bfloat16)
        kept_ref[pl.ds(at, size), :] = token_rows
        here = pl.ds(at, size)
        table_ref[:, here] = jnp.broadcast_to(nothing, (table_ref.shape[0], size))
        for slot, best in zip(ids, page_best(token_rows, pages_ref, tails)):
            row = pl.ds(slot, 1)
            table_ref[row, here] = jnp.maximum(table_ref[row, here], best)

    over_tiles(firsts[-1], visit)
    for spec, first in zip(specs, firsts):
        value = from_column(table_ref, first, span)
        to = column(spec)
        for distance in range(SPILL + 1):
            outs[distance][:, pl.ds(to, span)] = value[distance * docs : (distance + 1) * docs]


def home_kernel(
    specs, queries, plan_ref, kept_ref, all_pages_ref, before_ref, out_ref, tail_ref, table_ref
):
    docs, span = out_ref.shape[1:]
    pages_ref = all_pages_ref.at[pl.ds(0, docs)]
    x, c = own_position()
    ids = [plan_ref[queries + k] for k in range(docs)]
    tails = fill_tails(pages_ref, tail_ref)
    chunks = [chunk_of(spec, x, c) for spec in specs]
    firsts = [0]
    for chunk in chunks:
        firsts.append(firsts[-1] + chunk_count(plan_ref, chunk))

    def visit(at, size):
        here = pl.ds(at, size)
        table_ref[:, here] = jnp.full((table_ref.shape[0], size), lowest, jnp.float32)
        for slot, best in zip(ids, page_best(kept_ref[here, :], pages_ref, tails)):
            row = pl.ds(slot, 1)
            table_ref[row, here] = jnp.maximum(table_ref[row, here], best)

    over_tiles(firsts[-1], visit)
    for i, (chunk, first) in enumerate(zip(chunks, firsts)):
        value = from_column(table_ref, first, span)
        to = pl.multiple_of((chunk[0] * NC + chunk[1]) * span, TILE)
        out_ref[i] = jnp.maximum(before_ref[:, pl.ds(to, span)], value[:docs])


def scores_kernel(groups, plan_ref, lens_ref, chosen_ref, *rest):
    homes, rest = rest[: len(groups)], rest[len(groups) :]
    received, (out_ref, acc_ref) = rest[:SPILL], rest[SPILL:]
    docs, columns_all = received[0].shape
    lens = lens_ref[...]
    span = columns_all // (NX * NC)
    x, c = own_position()
    acc_ref[...] = jnp.zeros(acc_ref.shape, jnp.float32)
    parts_list = [
        (home, i, chunk_of(spec, x, c))
        for home, group in zip(homes, groups)
        for i, spec in enumerate(group)
    ]

    def visit(at, size):
        added = []
        for home_ref, i, chunk in parts_list:
            to = pl.multiple_of((chunk[0] * NC + chunk[1]) * span + at, TILE)
            live = lax.broadcasted_iota(jnp.int32, (docs, size), 1) + at < chunk_count(
                plan_ref, chunk
            )
            value = home_ref[i, :, pl.ds(at, size)]
            for ref in received:
                value = jnp.maximum(value, ref[:, pl.ds(to, size)])
            value = jnp.where(live, value, 0.0)
            value = jnp.concatenate([value, jnp.zeros((8 - docs, size), jnp.float32)], axis=0)
            high = value.astype(jnp.bfloat16).astype(jnp.float32)
            left = value - high
            middle = left.astype(jnp.bfloat16).astype(jnp.float32)
            pieces = [high, middle, left - middle, jnp.zeros((8, size), jnp.float32)]
            left_side = jnp.concatenate(pieces, axis=0).astype(jnp.bfloat16)
            added.append(
                jnp.dot(
                    left_side, chosen_ref[pl.ds(to, size), :], preferred_element_type=jnp.float32
                )
            )
        for (_, _, chunk), value in zip(parts_list, added):
            acc_ref[chunk[0] // 2] = acc_ref[chunk[0] // 2] + value

    tiles = (most_tokens(plan_ref) + TILE - 1) // TILE

    @pl.when(tiles >= 2)
    def _():
        visit(0, 2 * TILE)

    @pl.when(tiles % 2 == 1)
    def _():
        visit(pl.multiple_of((tiles - 1) * TILE, TILE), TILE)

    half = acc_ref.shape[2]
    for x_hi in range(acc_ref.shape[0]):
        lanes = slice(x_hi * half, (x_hi + 1) * half)
        divisor = lens[:, lanes].astype(jnp.float32)
        high, middle, low = (acc_ref[x_hi, 8 * i : 8 * i + docs, :] for i in range(3))
        out_ref[:, lanes] = ((high + middle) + low) / divisor


SMEM = pl.BlockSpec(memory_space=pltpu.SMEM)
VMEM = pl.BlockSpec(memory_space=pltpu.VMEM)
HBM = pl.BlockSpec(memory_space=pltpu.HBM)


def lowest_kernel(out_ref):
    out_ref[...] = jnp.full(out_ref.shape, lowest, jnp.float32)


def local(queries, query_len, pages, page_count, page_offset, helper_doc):
    docs = page_count.shape[0]
    total = query_len.shape[0]
    tokens, width = queries.shape[1:]
    columns = total * tokens
    span = columns // (NX * NC)
    room = span + TILE
    params = pltpu.CompilerParams(vmem_limit_bytes=VMEM_LIMIT)
    whole = [jax.ShapeDtypeStruct((docs, columns), jnp.float32)] * (SPILL + 1)
    slots = pltpu.VMEM((16, WIDE), jnp.float32)
    notes = pltpu.SMEM((16,), jnp.int32)
    row = query_len[None, :]
    own, far, rest = [(0, 0), (0, 1)], [(2, 0)], [(2, 1), (1, 0), (1, 1), (3, 0), (3, 1)]
    pool = len(rest) * span + 2 * WIDE

    def part(specs):
        return [jax.ShapeDtypeStruct((len(specs), docs, span), jnp.float32)] * (SPILL + 1)

    def tail_room(count):
        return pltpu.VMEM((8 * count + 8 * count % 16, width), jnp.float32)

    def live_room(specs):
        return pltpu.VMEM((len(specs) * room, width), jnp.float32)

    def cost(rows):
        return pl.CostEstimate(
            flops=2 * rows * columns * width, bytes_accessed=rows * width * 2, transcendentals=0
        )

    nothing = pl.pallas_call(
        lowest_kernel,
        out_shape=jax.ShapeDtypeStruct((8, 128), jnp.float32),
        out_specs=VMEM,
        cost_estimate=cost(pages.shape[0] * pages.shape[1]),
    )()
    queries, nothing = lax.optimization_barrier((queries, nothing))
    copies = jnp.broadcast_to(queries, (CHUNK, tokens, width))
    mine = lax.all_to_all(copies, ("y", "z"), 0, 0, tiled=True)
    mine_other = other_core(mine)
    two, three, one = [along_x(mine, steps) for steps in (2, 3, 1)]

    *own_out, plan = pl.pallas_call(
        functools.partial(first_kernel, own),
        out_shape=part(own)
        + [jax.ShapeDtypeStruct((total + pages.shape[0] + NX * NC,), jnp.int32)],
        in_specs=[HBM] * 4 + [VMEM] * (len(own) + 1),
        out_specs=[VMEM] * (SPILL + 1) + [SMEM],
        scratch_shapes=[
            pltpu.SMEM(page_count.shape, jnp.int32),
            pltpu.SMEM(page_offset.shape, jnp.int32),
            pltpu.SMEM(helper_doc.shape, jnp.int32),
            live_room(own),
            tail_room(pages.shape[0]),
            slots,
            notes,
            pltpu.SemaphoreType.DMA((4,)),
        ],
        compiler_params=params,
        cost_estimate=cost(700),
    )(query_len, page_count, page_offset, helper_doc, mine, mine_other, pages)

    two, plan = lax.optimization_barrier((two, plan))
    far_out = pl.pallas_call(
        functools.partial(more_kernel, far, total),
        out_shape=part(far),
        in_specs=[SMEM] + [VMEM] * (len(far) + 1),
        out_specs=[VMEM] * (SPILL + 1),
        scratch_shapes=[live_room(far), tail_room(pages.shape[0]), slots, notes],
        compiler_params=params,
        cost_estimate=cost(700),
    )(plan, two, pages)

    one, two, three, far_out = lax.optimization_barrier((one, two, three, far_out))
    two_other, one_other, three_other = [other_core(value) for value in (two, one, three)]
    chosen = pl.pallas_call(
        chosen_kernel,
        out_shape=jax.ShapeDtypeStruct((columns, total // 2), jnp.bfloat16),
        in_specs=[SMEM, VMEM],
        out_specs=VMEM,
        compiler_params=params,
        cost_estimate=cost(pages.shape[1]),
    )(plan, row)
    arrived = [two_other, one, one_other, three, three_other]
    *arrived, chosen = lax.optimization_barrier((*arrived, chosen))

    *partials, kept = pl.pallas_call(
        functools.partial(late_kernel, rest, (own, far), total),
        out_shape=whole + [jax.ShapeDtypeStruct((pool, width), jnp.bfloat16)],
        in_specs=[SMEM] + [VMEM] * (len(rest) + 2 + 2 * (SPILL + 1)),
        out_specs=[VMEM] * (SPILL + 2),
        scratch_shapes=[
            pltpu.VMEM((pool, width), jnp.float32),
            tail_room(pages.shape[0] - docs),
            pltpu.VMEM((16, pool), jnp.float32),
        ],
        compiler_params=params,
        cost_estimate=cost((pages.shape[0] - docs) * pages.shape[1]),
    )(plan, nothing, *arrived, pages, *own_out, *far_out)
    received = [along_blk(partials[distance], -distance) for distance in SEND_ORDER]

    rest_home = pl.pallas_call(
        functools.partial(home_kernel, rest, total),
        out_shape=part(rest)[0],
        in_specs=[SMEM] + [VMEM] * 3,
        out_specs=VMEM,
        scratch_shapes=[tail_room(docs), pltpu.VMEM((8, pool), jnp.float32)],
        compiler_params=params,
        cost_estimate=cost(docs * pages.shape[1]),
    )(plan, kept, pages, partials[0])

    return pl.pallas_call(
        functools.partial(scores_kernel, (own, far, rest)),
        out_shape=jax.ShapeDtypeStruct((docs, total), jnp.float32),
        in_specs=[SMEM] + [VMEM] * (SPILL + 5),
        out_specs=VMEM,
        scratch_shapes=[pltpu.VMEM((2, 32, total // 2), jnp.float32)],
        compiler_params=params,
    )(plan, row, chosen, own_out[0], far_out[0], rest_home, *received)


def solution(mesh):
    split = Mesh(mesh.devices.reshape(SIZES), AXES)
    return jax.shard_map(
        local,
        mesh=split,
        in_specs=(P(AXES, None, None), P(), P(AXES, None, None), P(AXES), P(AXES), P(AXES)),
        out_specs=P(AXES, None),
        check_vma=False,
    )
```

```python
import functools

import jax
import jax.numpy as jnp
from jax import lax
from jax.experimental import pallas as pl
from jax.experimental.pallas import tpu as pltpu
from jax.sharding import Mesh, PartitionSpec as P

SPILL = 3
SEND_ORDER = (3, 1, 2)
SIZES = (2, 4, 2, 8, 2)
AXES = ("xh", "y", "xl", "z", "c")
NX, NY, NZ, NC = 4, 4, 8, 2
CHUNK = NY * NZ
TILE = 256
WIDE = 2 * TILE
lowest = -1e30
VMEM_LIMIT = 48 * 1024 * 1024
TRANSPOSED = (((1,), (1,)), ((), ()))


def device_id(x, y, z, c):
    return (((x // 2) * NY + y) * 2 + x % 2) * NZ * NC + z * NC + c


def coordinates():
    return [
        (x, y, z, c) for x in range(NX) for y in range(NY) for z in range(NZ) for c in range(NC)
    ]


def along_x(value, steps):
    pairs = [
        (device_id(x, y, z, c), device_id((x + steps) % NX, y, z, c)) for x, y, z, c in coordinates()
    ]
    return lax.ppermute(value, AXES, pairs)


def other_core(value):
    pairs = [(device_id(x, y, z, c), device_id(x, y, z, 1 - c)) for x, y, z, c in coordinates()]
    return lax.ppermute(value, AXES, pairs)


def along_blk(value, steps):
    count = 32
    pairs = [
        (g * count + b, g * count + (b + steps) % count) for g in range(8) for b in range(count)
    ]
    return lax.ppermute(value, AXES, pairs)


def region_of(x_abs, core):
    return (x_abs // 2) * (NY * 2 * NZ * NC) + (x_abs % 2) * (NZ * NC) + core


PLACES = [y * (2 * NZ * NC) + z * NC for y in range(NY) for z in range(NZ)]


def chunk_total(len_ref, x_abs, core):
    first = region_of(x_abs, core)
    terms = [len_ref[first + place] for place in PLACES]
    while len(terms) > 1:
        terms = [sum(terms[i : i + 2]) for i in range(0, len(terms), 2)]
    return terms[0]


def chunk_of(spec, x, c):
    steps, core = spec
    return lax.rem(x + NX - steps, NX), (c if core == 0 else 1 - c)


def compact(len_ref, live_ref, base, chunk, source):
    tokens = source.shape[1]
    first = region_of(*chunk)
    at = base
    for k, place in enumerate(PLACES):
        live_ref[pl.ds(at, tokens), :] = source[k].astype(jnp.float32)
        at = at + len_ref[first + place]
    return at - base


def slot_ids(count_ref, offset_ref, helper_ref, pages):
    docs = count_ref.shape[0]
    ids = []
    for k in pages:
        slot = jnp.int32(0) if helper_ref is None else helper_ref[k]
        for j in range(docs):
            inside = (offset_ref[j] <= k) & (k < offset_ref[j] + count_ref[j])
            slot = jnp.where(inside, j, slot)
        ids.append(jnp.clip(slot, 0, (SPILL + 1) * docs - 1))
    return ids


def fill_tails(pages_ref, tail_ref):
    pages, patches, _ = pages_ref.shape
    whole = patches // 16 * 16
    tail_ref[...] = jnp.zeros(tail_ref.shape, jnp.float32)
    for p in range(pages):
        tail_ref[8 * p : 8 * p + patches - whole, :] = pages_ref[p, whole:, :].astype(jnp.float32)
        for extra in range(patches - whole, 8):
            tail_ref[8 * p + extra : 8 * p + extra + 1, :] = pages_ref[
                p, patches - 1 : patches, :
            ].astype(jnp.float32)
    return tail_ref[...].astype(jnp.bfloat16)


def page_best(token_rows, pages_ref, tails):
    pages, patches, _ = pages_ref.shape
    whole = patches // 16 * 16
    columns = token_rows.shape[0]
    tail_scores = lax.dot_general(
        tails, token_rows, TRANSPOSED, preferred_element_type=jnp.float32
    )
    rows = []
    for p in range(pages):
        scores = lax.dot_general(
            pages_ref[p, :whole, :], token_rows, TRANSPOSED, preferred_element_type=jnp.float32
        )
        best = jnp.max(scores.reshape(whole // 8, 8, columns), axis=0)
        best = jnp.maximum(best, tail_scores[8 * p : 8 * p + 8])
        rows.append(jnp.max(best, axis=0, keepdims=True))
    return rows


def over_tiles(total, visit):
    tiles = (total + TILE - 1) // TILE

    def four(i, _):
        visit(pl.multiple_of(i * (4 * TILE), 4 * TILE), 4 * TILE)
        return 0

    lax.fori_loop(0, tiles // 4, four, 0)
    done = tiles // 4 * 4

    @pl.when(tiles % 4 >= 2)
    def _():
        visit(pl.multiple_of(done * TILE, 4 * TILE), 2 * TILE)

    @pl.when(tiles % 2 == 1)
    def _():
        visit(pl.multiple_of((tiles - 1) * TILE, TILE), TILE)


def from_column(table_ref, first, span):
    if isinstance(first, int):
        return table_ref[:, first : first + span]
    lanes = 128
    base = pl.multiple_of(first // lanes * lanes, lanes)
    window = table_ref[:, pl.ds(base, span + lanes)]
    return pltpu.roll(window, lax.rem(span + lanes - (first - base), span + lanes), 1)[:, :span]


def own_position():
    return lax.axis_index("xh") * 2 + lax.axis_index("xl"), lax.axis_index("c")


def over_chunks(count, total_of, span, visit):
    def each(i, _):
        def tile(k, _):
            visit(i, pl.multiple_of(jnp.minimum(k * WIDE, span - WIDE), TILE))
            return 0

        lax.fori_loop(0, (total_of(i) + WIDE - 1) // WIDE, tile, 0)
        return 0

    lax.fori_loop(0, count, each, 0)


def whole_chunks(specs, plan_ref, sources, outs, pages_ref, live_ref, slot_ref, note_ref, ids, tails):
    x, c = own_position()
    room = live_ref.shape[0] // len(specs)
    for i, (spec, source) in enumerate(zip(specs, sources)):
        note_ref[i] = compact(plan_ref, live_ref, i * room, chunk_of(spec, x, c), source)

    docs, span = outs[0].shape[1:]

    def visit(i, at):
        base = pl.multiple_of(i * room, TILE)
        token_rows = live_ref[pl.ds(base + at, WIDE), :].astype(jnp.bfloat16)
        slot_ref[...] = jnp.full(slot_ref.shape, lowest, jnp.float32)
        for slot, best in zip(ids, page_best(token_rows, pages_ref, tails)):
            row = pl.ds(slot, 1)
            slot_ref[row, :] = jnp.maximum(slot_ref[row, :], best)
        for distance in range(SPILL + 1):
            outs[distance][i, :, pl.ds(at, WIDE)] = slot_ref[
                distance * docs : (distance + 1) * docs, :
            ]

    over_chunks(len(specs), lambda i: note_ref[i], span, visit)


def first_kernel(specs, len_hbm, count_hbm, offset_hbm, helper_hbm, *rest):
    sources, rest = rest[: len(specs)], rest[len(specs) :]
    pages_ref, rest = rest[0], rest[1:]
    outs, rest = rest[: SPILL + 1], rest[SPILL + 1 :]
    plan_ref, count_ref, offset_ref, helper_ref, live_ref, tail_ref, slot_ref, note_ref, sem = rest
    pages = pages_ref.shape[0]
    moves = [
        pltpu.make_async_copy(source, target, sem.at[i])
        for i, (source, target) in enumerate(
            (
                (len_hbm, plan_ref.at[pl.ds(0, len_hbm.shape[0])]),
                (count_hbm, count_ref),
                (offset_hbm, offset_ref),
                (helper_hbm, helper_ref),
            )
        )
    ]
    for move in moves:
        move.start()
    tails = fill_tails(pages_ref, tail_ref)
    for move in moves:
        move.wait()
    ids = slot_ids(count_ref, offset_ref, helper_ref, range(pages))
    at = len_hbm.shape[0]
    for k in range(pages):
        plan_ref[at + k] = ids[k]
    for chunk in range(NX * NC):
        plan_ref[at + pages + chunk] = chunk_total(plan_ref, chunk // NC, chunk % NC)
    whole_chunks(specs, plan_ref, sources, outs, pages_ref, live_ref, slot_ref, note_ref, ids, tails)


def more_kernel(specs, queries, plan_ref, *rest):
    sources, rest = rest[: len(specs)], rest[len(specs) :]
    pages_ref, rest = rest[0], rest[1:]
    outs, rest = rest[: SPILL + 1], rest[SPILL + 1 :]
    live_ref, tail_ref, slot_ref, note_ref = rest
    ids = [plan_ref[queries + k] for k in range(pages_ref.shape[0])]
    tails = fill_tails(pages_ref, tail_ref)
    whole_chunks(specs, plan_ref, sources, outs, pages_ref, live_ref, slot_ref, note_ref, ids, tails)


def chunk_count(plan_ref, chunk):
    return plan_ref[plan_ref.shape[0] - NX * NC + chunk[0] * NC + chunk[1]]


def most_tokens(plan_ref):
    most = plan_ref[plan_ref.shape[0] - NX * NC]
    for chunk in range(1, NX * NC):
        most = jnp.maximum(most, plan_ref[plan_ref.shape[0] - NX * NC + chunk])
    return most


def chosen_kernel(plan_ref, lens_ref, chosen_ref):
    span = chosen_ref.shape[0] // (NX * NC)
    half = chosen_ref.shape[1]
    starts, ends = query_columns(lens_ref[...], span)

    def step(tile, _):
        for chunk in range(NX * NC):
            lanes = slice(chunk // (2 * NC) * half, (chunk // (2 * NC) + 1) * half)
            first = pl.multiple_of(chunk * span + tile * TILE, TILE)
            token = lax.broadcasted_iota(jnp.int32, (TILE, half), 0) + first
            inside = (token >= starts[:, lanes]) & (token < ends[:, lanes])
            chosen_ref[pl.ds(first, TILE), :] = jnp.where(inside, 1.0, 0.0).astype(jnp.bfloat16)
        return 0

    lax.fori_loop(0, (most_tokens(plan_ref) + TILE - 1) // TILE, step, 0)


def query_columns(lens, span):
    queries = lens.shape[1]

    def chunk(n):
        return ((n // (NC * NZ * 2 * NY)) * 2 + (n // (NC * NZ)) % 2) * NC + n % NC

    def place(n):
        return (n // (NC * NZ * 2)) % NY * NZ + (n // NC) % NZ

    one = lax.broadcasted_iota(jnp.int32, (queries, queries), 0)
    two = lax.broadcasted_iota(jnp.int32, (queries, queries), 1)
    before = (chunk(one) == chunk(two)) & (place(one) < place(two))
    row = jnp.broadcast_to(lens.astype(jnp.float32).astype(jnp.bfloat16), (16, queries))
    starts = jnp.dot(
        row,
        jnp.where(before, 1.0, 0.0).astype(jnp.bfloat16),
        preferred_element_type=jnp.float32,
    )[0:1].astype(jnp.int32)
    starts = starts + chunk(lax.broadcasted_iota(jnp.int32, (1, queries), 1)) * span
    return starts, starts + lens


def late_kernel(specs, placed, queries, plan_ref, nothing_ref, *rest):
    sources, rest = rest[: len(specs)], rest[len(specs) :]
    all_pages_ref, rest = rest[0], rest[1:]
    before, rest = rest[: len(placed) * (SPILL + 1)], rest[len(placed) * (SPILL + 1) :]
    outs, rest = rest[: SPILL + 1], rest[SPILL + 1 :]
    kept_ref, live_ref, tail_ref, table_ref = rest
    docs, columns_all = outs[0].shape
    pages = all_pages_ref.shape[0]
    pages_ref = all_pages_ref.at[pl.ds(docs, pages - docs)]
    x, c = own_position()
    span = columns_all // (NX * NC)

    def column(spec):
        chunk = chunk_of(spec, x, c)
        return pl.multiple_of((chunk[0] * NC + chunk[1]) * span, TILE)

    for group, group_specs in enumerate(placed):
        for i, spec in enumerate(group_specs):
            for distance in range(SPILL + 1):
                outs[distance][:, pl.ds(column(spec), span)] = before[
                    group * (SPILL + 1) + distance
                ][i]
    ids = [plan_ref[queries + k] for k in range(docs, pages)]
    tails = fill_tails(pages_ref, tail_ref)
    firsts = [0]
    for spec, source in zip(specs, sources):
        chunk = chunk_of(spec, x, c)
        compact(plan_ref, live_ref, firsts[-1], chunk, source)
        firsts.append(firsts[-1] + chunk_count(plan_ref, chunk))

    nothing = nothing_ref[0:1, 0:1]

    def visit(at, size):
        token_rows = live_ref[pl.ds(at, size), :].astype(jnp.bfloat16)
        kept_ref[pl.ds(at, size), :] = token_rows
        here = pl.ds(at, size)
        table_ref[:, here] = jnp.broadcast_to(nothing, (table_ref.shape[0], size))
        for slot, best in zip(ids, page_best(token_rows, pages_ref, tails)):
            row = pl.ds(slot, 1)
            table_ref[row, here] = jnp.maximum(table_ref[row, here], best)

    over_tiles(firsts[-1], visit)
    for spec, first in zip(specs, firsts):
        value = from_column(table_ref, first, span)
        to = column(spec)
        for distance in range(SPILL + 1):
            outs[distance][:, pl.ds(to, span)] = value[distance * docs : (distance + 1) * docs]


def home_kernel(
    specs, queries, plan_ref, kept_ref, all_pages_ref, before_ref, out_ref, tail_ref, table_ref
):
    docs, span = out_ref.shape[1:]
    pages_ref = all_pages_ref.at[pl.ds(0, docs)]
    x, c = own_position()
    ids = [plan_ref[queries + k] for k in range(docs)]
    tails = fill_tails(pages_ref, tail_ref)
    chunks = [chunk_of(spec, x, c) for spec in specs]
    firsts = [0]
    for chunk in chunks:
        firsts.append(firsts[-1] + chunk_count(plan_ref, chunk))

    def visit(at, size):
        here = pl.ds(at, size)
        table_ref[:, here] = jnp.full((table_ref.shape[0], size), lowest, jnp.float32)
        for slot, best in zip(ids, page_best(kept_ref[here, :], pages_ref, tails)):
            row = pl.ds(slot, 1)
            table_ref[row, here] = jnp.maximum(table_ref[row, here], best)

    over_tiles(firsts[-1], visit)
    for i, (chunk, first) in enumerate(zip(chunks, firsts)):
        value = from_column(table_ref, first, span)
        to = pl.multiple_of((chunk[0] * NC + chunk[1]) * span, TILE)
        out_ref[i] = jnp.maximum(before_ref[:, pl.ds(to, span)], value[:docs])


def scores_kernel(groups, plan_ref, lens_ref, chosen_ref, *rest):
    homes, rest = rest[: len(groups)], rest[len(groups) :]
    received, (out_ref, acc_ref) = rest[:SPILL], rest[SPILL:]
    docs, columns_all = received[0].shape
    lens = lens_ref[...]
    span = columns_all // (NX * NC)
    x, c = own_position()
    acc_ref[...] = jnp.zeros(acc_ref.shape, jnp.float32)
    parts_list = [
        (home, i, chunk_of(spec, x, c))
        for home, group in zip(homes, groups)
        for i, spec in enumerate(group)
    ]

    def visit(at, size):
        added = []
        for home_ref, i, chunk in parts_list:
            to = pl.multiple_of((chunk[0] * NC + chunk[1]) * span + at, TILE)
            live = lax.broadcasted_iota(jnp.int32, (docs, size), 1) + at < chunk_count(
                plan_ref, chunk
            )
            value = home_ref[i, :, pl.ds(at, size)]
            for ref in received:
                value = jnp.maximum(value, ref[:, pl.ds(to, size)])
            value = jnp.where(live, value, 0.0)
            value = jnp.concatenate([value, jnp.zeros((8 - docs, size), jnp.float32)], axis=0)
            high = value.astype(jnp.bfloat16).astype(jnp.float32)
            left = value - high
            middle = left.astype(jnp.bfloat16).astype(jnp.float32)
            pieces = [high, middle, left - middle, jnp.zeros((8, size), jnp.float32)]
            left_side = jnp.concatenate(pieces, axis=0).astype(jnp.bfloat16)
            added.append(
                jnp.dot(
                    left_side, chosen_ref[pl.ds(to, size), :], preferred_element_type=jnp.float32
                )
            )
        for (_, _, chunk), value in zip(parts_list, added):
            acc_ref[chunk[0] // 2] = acc_ref[chunk[0] // 2] + value

    tiles = (most_tokens(plan_ref) + TILE - 1) // TILE

    @pl.when(tiles >= 2)
    def _():
        visit(0, 2 * TILE)

    @pl.when(tiles % 2 == 1)
    def _():
        visit(pl.multiple_of((tiles - 1) * TILE, TILE), TILE)

    half = acc_ref.shape[2]
    for x_hi in range(acc_ref.shape[0]):
        lanes = slice(x_hi * half, (x_hi + 1) * half)
        divisor = lens[:, lanes].astype(jnp.float32)
        high, middle, low = (acc_ref[x_hi, 8 * i : 8 * i + docs, :] for i in range(3))
        out_ref[:, lanes] = ((high + middle) + low) / divisor


SMEM = pl.BlockSpec(memory_space=pltpu.SMEM)
VMEM = pl.BlockSpec(memory_space=pltpu.VMEM)
HBM = pl.BlockSpec(memory_space=pltpu.HBM)


def lowest_kernel(out_ref):
    out_ref[...] = jnp.full(out_ref.shape, lowest, jnp.float32)


def local(queries, query_len, pages, page_count, page_offset, helper_doc):
    docs = page_count.shape[0]
    total = query_len.shape[0]
    tokens, width = queries.shape[1:]
    columns = total * tokens
    span = columns // (NX * NC)
    room = span + TILE
    params = pltpu.CompilerParams(vmem_limit_bytes=VMEM_LIMIT)
    whole = [jax.ShapeDtypeStruct((docs, columns), jnp.float32)] * (SPILL + 1)
    slots = pltpu.VMEM((16, WIDE), jnp.float32)
    notes = pltpu.SMEM((16,), jnp.int32)
    row = query_len[None, :]
    own, far, rest = [(0, 0), (0, 1)], [(2, 0)], [(2, 1), (1, 0), (1, 1), (3, 0), (3, 1)]
    pool = len(rest) * span + 2 * WIDE

    def part(specs):
        return [jax.ShapeDtypeStruct((len(specs), docs, span), jnp.float32)] * (SPILL + 1)

    def tail_room(count):
        return pltpu.VMEM((8 * count + 8 * count % 16, width), jnp.float32)

    def live_room(specs):
        return pltpu.VMEM((len(specs) * room, width), jnp.float32)

    def cost(rows):
        return pl.CostEstimate(
            flops=2 * rows * columns * width, bytes_accessed=rows * width * 2, transcendentals=0
        )

    nothing = pl.pallas_call(
        lowest_kernel,
        out_shape=jax.ShapeDtypeStruct((8, 128), jnp.float32),
        out_specs=VMEM,
        cost_estimate=cost(pages.shape[0] * pages.shape[1]),
    )()
    queries, nothing = lax.optimization_barrier((queries, nothing))
    copies = jnp.broadcast_to(queries, (CHUNK, tokens, width))
    mine = lax.all_to_all(copies, ("y", "z"), 0, 0, tiled=True)
    mine_other = other_core(mine)
    two, three, one = [along_x(mine, steps) for steps in (2, 3, 1)]

    *own_out, plan = pl.pallas_call(
        functools.partial(first_kernel, own),
        out_shape=part(own)
        + [jax.ShapeDtypeStruct((total + pages.shape[0] + NX * NC,), jnp.int32)],
        in_specs=[HBM] * 4 + [VMEM] * (len(own) + 1),
        out_specs=[VMEM] * (SPILL + 1) + [SMEM],
        scratch_shapes=[
            pltpu.SMEM(page_count.shape, jnp.int32),
            pltpu.SMEM(page_offset.shape, jnp.int32),
            pltpu.SMEM(helper_doc.shape, jnp.int32),
            live_room(own),
            tail_room(pages.shape[0]),
            slots,
            notes,
            pltpu.SemaphoreType.DMA((4,)),
        ],
        compiler_params=params,
        cost_estimate=cost(700),
    )(query_len, page_count, page_offset, helper_doc, mine, mine_other, pages)

    two, plan = lax.optimization_barrier((two, plan))
    far_out = pl.pallas_call(
        functools.partial(more_kernel, far, total),
        out_shape=part(far),
        in_specs=[SMEM] + [VMEM] * (len(far) + 1),
        out_specs=[VMEM] * (SPILL + 1),
        scratch_shapes=[live_room(far), tail_room(pages.shape[0]), slots, notes],
        compiler_params=params,
        cost_estimate=cost(700),
    )(plan, two, pages)

    one, two, three, far_out = lax.optimization_barrier((one, two, three, far_out))
    three_other, one_other, two_other = [other_core(value) for value in (three, one, two)]
    chosen = pl.pallas_call(
        chosen_kernel,
        out_shape=jax.ShapeDtypeStruct((columns, total // 2), jnp.bfloat16),
        in_specs=[SMEM, VMEM],
        out_specs=VMEM,
        compiler_params=params,
        cost_estimate=cost(pages.shape[1]),
    )(plan, row)
    arrived = [two_other, one, one_other, three, three_other]
    *arrived, chosen = lax.optimization_barrier((*arrived, chosen))

    *partials, kept = pl.pallas_call(
        functools.partial(late_kernel, rest, (own, far), total),
        out_shape=whole + [jax.ShapeDtypeStruct((pool, width), jnp.bfloat16)],
        in_specs=[SMEM] + [VMEM] * (len(rest) + 2 + 2 * (SPILL + 1)),
        out_specs=[VMEM] * (SPILL + 2),
        scratch_shapes=[
            pltpu.VMEM((pool, width), jnp.float32),
            tail_room(pages.shape[0] - docs),
            pltpu.VMEM((16, pool), jnp.float32),
        ],
        compiler_params=params,
        cost_estimate=cost((pages.shape[0] - docs) * pages.shape[1]),
    )(plan, nothing, *arrived, pages, *own_out, *far_out)
    received = [along_blk(partials[distance], -distance) for distance in SEND_ORDER]

    rest_home = pl.pallas_call(
        functools.partial(home_kernel, rest, total),
        out_shape=part(rest)[0],
        in_specs=[SMEM] + [VMEM] * 3,
        out_specs=VMEM,
        scratch_shapes=[tail_room(docs), pltpu.VMEM((8, pool), jnp.float32)],
        compiler_params=params,
        cost_estimate=cost(docs * pages.shape[1]),
    )(plan, kept, pages, partials[0])

    return pl.pallas_call(
        functools.partial(scores_kernel, (own, far, rest)),
        out_shape=jax.ShapeDtypeStruct((docs, total), jnp.float32),
        in_specs=[SMEM] + [VMEM] * (SPILL + 5),
        out_specs=VMEM,
        scratch_shapes=[pltpu.VMEM((2, 32, total // 2), jnp.float32)],
        compiler_params=params,
    )(plan, row, chosen, own_out[0], far_out[0], rest_home, *received)


def solution(mesh):
    split = Mesh(mesh.devices.reshape(SIZES), AXES)
    return jax.shard_map(
        local,
        mesh=split,
        in_specs=(P(AXES, None, None), P(), P(AXES, None, None), P(AXES), P(AXES), P(AXES)),
        out_specs=P(AXES, None),
        check_vma=False,
    )
```
